256 devices in a mesh: dp: 8 (over z), ctx: 32 (over y, x, core).
Axes of the slice: x: 4, y: 4, z: 8, core: 2. Of those that a mesh axis runs over, the one named last changes fastest.
Arguments:
- output_gate_input: bfloat16 [8, 4096, 4096], P('dp', 'ctx'), may hold values from -6 to 6
- key_input: bfloat16 [8, 4096, 4096], P('dp', 'ctx'), may hold values from -6 to 6
- value_input: bfloat16 [8, 4096, 4096], P('dp', 'ctx'), may hold values from -6 to 6
- upstream: bfloat16 [8, 4096, 4096], P('dp', 'ctx'), may hold values from -6 to 6
- filter_taps: float32 [256, 4096], P('ctx'), may hold values from -6 to 6
- block_of_shard: int32 [32], replicated, may hold values from 0 to 31, each once
Outputs:
- mixed_out: bfloat16 [8, 4096, 4096], P('dp', 'ctx')
- gate_grad: bfloat16 [8, 4096, 4096], P('dp', 'ctx')
- key_grad: bfloat16 [8, 4096, 4096], P('dp', 'ctx')
- value_grad: bfloat16 [8, 4096, 4096], P('dp', 'ctx')
- taps_grad: float32 [256, 4096], P('ctx')
The draws below stay inside these ranges and needn't reach their ends.
Inputs may be any that keep to these rules, and one draw needn't show every extreme that they name: block_of_shard names every block of positions exactly once.
All inputs are finite; a program needn't handle non-finite values.
Results may differ from the reference program's by a relative error of at most 0.012.
Values may be sent and summed in bfloat16 or wider, within the bound.
No kernel may reach another device: no remote copies, remote signals or barrier semaphores. Data moves between devices by JAX's collectives and lax.ppermute only.
A program may use at most 192 MiB of HBM per device.

```python
import math
import jax
import jax.numpy as jnp
from jax import lax

D = 4096
GROUP = 16
SEQ = 4096
SEQS = 8
POSITION_BLOCKS = 32
FILTERS = 256
N_DP = 8


def draw_filter_taps(key, part):
    subkeys = jax.random.split(key, 6)
    delay_positions = jnp.arange(SEQ, dtype=jnp.float32)[None, :]
    decay_length = jnp.exp(jax.random.uniform(subkeys[1], (FILTERS, 1), minval=math.log(30.0), maxval=math.log(4.0 * SEQ)))
    base_vals = jax.random.truncated_normal(subkeys[3], -6.0, 6.0, (FILTERS, SEQ))
    token_positions = jax.random.randint(subkeys[4], (FILTERS, 3, 1), 1, SEQ).astype(jnp.float32)
    envelope_factors = jax.random.uniform(subkeys[5], (FILTERS, 3, 1), minval=0.5, maxval=0.8)
    spike_step_count = jnp.where(delay_positions[:, None, :] >= token_positions, envelope_factors, 1.0)
    decay_envelope = jnp.exp(-delay_positions / decay_length) * jnp.prod(spike_step_count, axis=1)
    return (base_vals * decay_envelope).astype(jnp.float32)


def levels(key, shape, cuts, least, largest):
    def one(axis_at, blocks):
        steps = jax.random.uniform(jax.random.fold_in(jax.random.fold_in(key, 6), axis_at), (blocks,), jnp.float32, least / len(cuts), largest / len(cuts))
        return jnp.repeat(jnp.exp(steps), shape[axis_at] // blocks).reshape((-1,) + (1,) * (len(shape) - axis_at - 1))

    gain = one(*cuts[0])
    for cut in cuts[1:]:
        gain = gain * one(*cut)
    return gain


def noise(own_key, extent, width, limit, cuts=(), kind=jnp.bfloat16):
    gain = levels(own_key, extent, cuts, -0.22, 0.18) if cuts else 1.0
    result = jax.random.normal(own_key, extent, jnp.float32) * width * gain
    return jnp.minimum(jnp.maximum(result, -limit), limit).astype(kind)


def setup_inputs(seed: int = 0) -> dict:
    splits = jax.random.split(jax.random.key(seed), 7)
    output_gate_input = noise(splits[0], (SEQS, SEQ, D), 1.0, 6.0, ((0, 8), (1, 32)))
    key_input = noise(splits[1], (SEQS, SEQ, D), 1.0, 6.0, ((0, 8), (1, 32)))
    value_input = noise(splits[2], (SEQS, SEQ, D), 1.0, 6.0, ((0, 8), (1, 32)))
    upstream = noise(splits[3], (SEQS, SEQ, D), 1.0, 6.0, ((0, 8), (1, 32)))
    filter_taps = draw_filter_taps(jax.random.fold_in(splits[6], 71), 0)
    block_of_shard = jax.random.permutation(splits[5], POSITION_BLOCKS).astype(jnp.int32)
    return dict(output_gate_input=output_gate_input, key_input=key_input, value_input=value_input, upstream=upstream, filter_taps=filter_taps, block_of_shard=block_of_shard)


epsilon = 1e-06

def inverse_order(block_of_shard):
    pieces = block_of_shard.shape[0]
    labels = jnp.arange(pieces, dtype=jnp.int32)
    matches = (block_of_shard[:, None] == labels[None, :]).astype(jnp.int32)
    return lax.optimization_barrier(jnp.sum(labels[:, None] * matches, axis=0)).astype(jnp.int32)

def reorder_blocks(row_data, placing):
    pieces = placing.shape[0]
    shaped = row_data.reshape((pieces, row_data.shape[0] // pieces) + row_data.shape[1:])
    return jnp.take(shaped, placing, axis=0).reshape(row_data.shape)

def rounded(values):
    return lax.optimization_barrier(values.astype(jnp.bfloat16)).astype(jnp.float32)

def reference(output_gate_input, key_input, value_input, upstream, filter_taps, block_of_shard):
    length = filter_taps.shape[1]
    filters = filter_taps.shape[0]
    inverse = inverse_order(block_of_shard)
    taps = filter_taps.astype(jnp.float32)
    root_mean = jnp.sqrt(lax.optimization_barrier(jnp.mean(taps * taps, axis=1, keepdims=True)) + epsilon)
    norm_scale = 1.0 / (math.sqrt(length) * root_mean)
    kernel = rounded(taps * norm_scale)
    kernel_freq = jnp.fft.rfft(jnp.repeat(kernel.T, GROUP, axis=1), n=2 * length, axis=0)

    def per_sequence(inputs):
        gates, keys_in, values_in, grads_up = [reorder_blocks(member, inverse).astype(jnp.float32) for member in inputs]
        product = rounded(keys_in * values_in)
        product_freq = jnp.fft.rfft(product, n=2 * length, axis=0)
        mixing = rounded(jnp.fft.irfft(product_freq * kernel_freq, n=2 * length, axis=0)[:length])
        weighted = rounded(grads_up * gates)
        weighted_freq = jnp.fft.rfft(weighted, n=2 * length, axis=0)
        returned = rounded(jnp.fft.irfft(jnp.conj(kernel_freq) * weighted_freq, n=2 * length, axis=0)[:length])
        lag_sums = jnp.fft.irfft(weighted_freq * jnp.conj(product_freq), n=2 * length, axis=0)[:length]
        lag_sums = lax.optimization_barrier(jnp.sum(lag_sums.reshape(length, filters, GROUP), axis=2)).T
        results = (gates * mixing, grads_up * mixing, returned * values_in, returned * keys_in)
        results = tuple((reorder_blocks(member.astype(jnp.bfloat16), block_of_shard) for member in results))
        return results + (lag_sums,)
    mixed, gate_grad, key_grad, value_grad, lag_all = lax.map(per_sequence, (output_gate_input, key_input, value_input, upstream))
    lag_mean = lax.optimization_barrier(jnp.sum(lag_all, axis=0)) / N_DP
    projection = lax.optimization_barrier(jnp.sum(lag_mean * taps, axis=1, keepdims=True))
    taps_grad = norm_scale * lag_mean - taps * (norm_scale * norm_scale * norm_scale) * projection
    return (mixed, gate_grad, key_grad, value_grad, taps_grad)
```

```python
import functools
import math

import jax
import jax.numpy as jnp
from jax import lax
from jax.experimental import pallas as pl
from jax.experimental.pallas import tpu as pltpu
from jax.sharding import PartitionSpec as P

EPSILON = 1e-06
BLOCK = 128
GROUP = 16
VMEM_LIMIT = 48 * 1024 * 1024

NN = (((1,), (0,)), ((), ()))
NT = (((1,), (1,)), ((), ()))
TN = (((0,), (0,)), ((), ()))


def dot(a, b, dims):
    return lax.dot_general(a, b, dims, preferred_element_type=jnp.float32)


def params():
    return pltpu.CompilerParams(vmem_limit_bytes=VMEM_LIMIT)


def product_of(a, b):
    return (a.astype(jnp.float32) * b.astype(jnp.float32)).astype(jnp.bfloat16)


def pre_kernel(tiles, a_ref, b_ref, out_ref):
    for i in range(tiles):
        cols = slice(i * BLOCK, (i + 1) * BLOCK)
        out_ref[i] = product_of(a_ref[0, :, cols], b_ref[0, :, cols]).T


def pre(a, b):
    _, rows, channels = a.shape
    pieces = channels // BLOCK
    tiles = 4
    spec = pl.BlockSpec((1, rows, tiles * BLOCK), lambda i: (0, 0, i))
    return pl.pallas_call(
        functools.partial(pre_kernel, tiles),
        grid=(pieces // tiles,),
        in_specs=[spec, spec],
        out_specs=pl.BlockSpec((tiles, BLOCK, rows), lambda i: (i, 0, 0)),
        out_shape=jax.ShapeDtypeStruct((pieces, BLOCK, rows), jnp.bfloat16),
        compiler_params=params(),
        cost_estimate=pl.CostEstimate(
            flops=a.size, bytes_accessed=6 * a.size, transcendentals=0
        ),
    )(a, b)


def strip_kernel(taps_ref, out_ref):
    g = pl.program_id(0)
    taps = taps_ref[pl.ds(g, 1), :]
    length = taps.shape[1]
    root = jnp.sqrt(jnp.mean(taps * taps, axis=1, keepdims=True) + EPSILON)
    row = taps * (1.0 / (math.sqrt(length) * root))
    width = length + BLOCK
    cur = jnp.concatenate([jnp.zeros((1, BLOCK), jnp.float32), row], axis=1)
    cur = jnp.broadcast_to(cur, (16, width))
    line = lax.broadcasted_iota(jnp.int32, (16, width), 0)
    for step in (1, 2, 4, 8):
        cur = jnp.where((line & step) != 0, pltpu.roll(cur, step, 1), cur)
    for q in range(BLOCK // 16):
        if q:
            cur = pltpu.roll(cur, 16, 1)
        out_ref[0, 16 * q : 16 * (q + 1), :] = cur.astype(jnp.bfloat16)
    out_ref[0, :, :BLOCK] = jnp.zeros((BLOCK, BLOCK), jnp.bfloat16)


def strips(taps):
    groups, length = taps.shape
    width = length + BLOCK
    return pl.pallas_call(
        strip_kernel,
        grid=(groups,),
        in_specs=[pl.BlockSpec((groups, length), lambda g: (0, 0))],
        out_specs=pl.BlockSpec((1, BLOCK, width), lambda g: (g, 0, 0)),
        out_shape=jax.ShapeDtypeStruct((groups, BLOCK, width), jnp.bfloat16),
        compiler_params=params(),
        cost_estimate=pl.CostEstimate(
            flops=4 * groups * BLOCK * width,
            bytes_accessed=2 * groups * BLOCK * width,
            transcendentals=0,
        ),
    )(taps)


def place(order_ref, from_ref, to_ref):
    for d in range(from_ref.shape[0]):
        b = order_ref[d]
        to_ref[b % 2, pl.ds(pl.multiple_of(GROUP * (b // 2), GROUP), GROUP), :] = from_ref[d]


def take(order_ref, from_ref, to_ref):
    for d in range(to_ref.shape[0]):
        b = order_ref[d]
        rows = pl.ds(pl.multiple_of(GROUP * (b // 2), GROUP), GROUP)
        to_ref[d] = from_ref[b % 2, rows, :].astype(jnp.bfloat16)


def conv_kernel(backward, order_ref, x_ref, strip_ref, out_ref, xs, acc):
    place(order_ref, x_ref, xs)
    rows = xs.shape[1]
    pairs = rows // GROUP
    for lag in range(pairs):
        at = BLOCK + 2 * BLOCK * lag
        weights = jnp.concatenate(
            [
                strip_ref[0, :, at : at + 2 * BLOCK],
                strip_ref[0, :, at - BLOCK : at + BLOCK],
            ],
            axis=0,
        )
        low, high = slice(0, rows - GROUP * lag), slice(GROUP * lag, rows)
        source, target = (high, low) if backward else (low, high)
        left = jnp.concatenate([xs[0, source, :], xs[1, source, :]], axis=1)
        part = dot(left, weights, NT if backward else NN)
        if lag == 0:
            acc[0] = part[:, :BLOCK]
            acc[1] = part[:, BLOCK:]
        else:
            acc[0, target, :] += part[:, :BLOCK]
            acc[1, target, :] += part[:, BLOCK:]
    take(order_ref, acc, out_ref)


def conv(order, x, strip, backward):
    pieces = x.shape[0]
    groups, _, width = strip.shape
    rows = GROUP * pieces // 2
    spec = pl.BlockSpec((pieces, GROUP, BLOCK), lambda g, order: (0, g, 0))
    return pl.pallas_call(
        functools.partial(conv_kernel, backward),
        grid_spec=pltpu.PrefetchScalarGridSpec(
            num_scalar_prefetch=1,
            grid=(groups,),
            in_specs=[
                spec,
                pl.BlockSpec((1, BLOCK, width), lambda g, order: (g, 0, 0)),
            ],
            out_specs=spec,
            scratch_shapes=[
                pltpu.VMEM((2, rows, BLOCK), jnp.bfloat16),
                pltpu.VMEM((2, rows, BLOCK), jnp.float32),
            ],
        ),
        out_shape=jax.ShapeDtypeStruct(x.shape, jnp.bfloat16),
        compiler_params=params(),
        cost_estimate=pl.CostEstimate(
            flops=groups * rows * rows * 16 * BLOCK,
            bytes_accessed=4 * x.size + 2 * strip.size,
            transcendentals=0,
        ),
    )(order, x, strip)


def lag_kernel(order_ref, x_ref, w_ref, out_ref, xs, ws, squares):
    pieces = x_ref.shape[0]
    total = GROUP * pieces
    for d in range(pieces):
        rows = pl.ds(pl.multiple_of(GROUP * order_ref[d], GROUP), GROUP)
        xs[rows, :] = x_ref[d]
        ws[rows, :] = w_ref[d]
    ws[total : total + GROUP, :] = jnp.zeros((GROUP, BLOCK), jnp.bfloat16)
    x_turned = xs[...].T
    for lag in range(0, pieces, 2):
        depth = total - GROUP * lag
        start = GROUP * lag
        right = jnp.concatenate(
            [ws[start : start + depth, :], ws[start + GROUP : start + GROUP + depth, :]],
            axis=1,
        )
        squares[:, lag * BLOCK : (lag + 2) * BLOCK] = dot(x_turned[:, :depth], right, NN)
    row = lax.broadcasted_iota(jnp.int32, (BLOCK, BLOCK), 0)
    col = lax.broadcasted_iota(jnp.int32, (BLOCK, BLOCK), 1)
    squares[:, :BLOCK] = jnp.where(col >= row, squares[:, :BLOCK], 0.0)
    width = squares.shape[1]
    cur = squares[BLOCK - 8 :, :]
    for q in range(BLOCK // 8 - 2, -1, -1):
        cur = pltpu.roll(cur, width - 8, 1) + squares[8 * q : 8 * (q + 1), :]
    line = lax.broadcasted_iota(jnp.int32, (8, width), 0)
    for step in (1, 2, 4):
        cur = jnp.where((line & step) != 0, pltpu.roll(cur, width - step, 1), cur)
    out_ref[pl.ds(pl.program_id(0), 1), :] = jnp.sum(cur, axis=0, keepdims=True)


def lag_sums_of(order, x, w, groups):
    pieces = x.shape[0]
    length = pieces * BLOCK
    rows = GROUP * pieces
    spec = pl.BlockSpec((pieces, GROUP, BLOCK), lambda g, order: (0, g, 0))
    return pl.pallas_call(
        lag_kernel,
        grid_spec=pltpu.PrefetchScalarGridSpec(
            num_scalar_prefetch=1,
            grid=(groups,),
            in_specs=[spec, spec],
            out_specs=pl.BlockSpec((groups, length), lambda g, order: (0, 0)),
            scratch_shapes=[
                pltpu.VMEM((rows, BLOCK), jnp.bfloat16),
                pltpu.VMEM((rows + GROUP, BLOCK), jnp.bfloat16),
                pltpu.VMEM((BLOCK, length), jnp.float32),
            ],
        ),
        out_shape=jax.ShapeDtypeStruct((groups, length), jnp.float32),
        compiler_params=params(),
        cost_estimate=pl.CostEstimate(
            flops=groups * rows * BLOCK * length,
            bytes_accessed=4 * x.size,
            transcendentals=0,
        ),
    )(order, x, w)


def post_kernel(tiles, r_ref, a_ref, b_ref, out_a_ref, out_b_ref):
    for i in range(tiles):
        cols = slice(i * BLOCK, (i + 1) * BLOCK)
        turned = r_ref[i].T
        out_a_ref[0, :, cols] = product_of(a_ref[0, :, cols], turned)
        out_b_ref[0, :, cols] = product_of(b_ref[0, :, cols], turned)


def post(r, a, b):
    _, rows, channels = a.shape
    pieces = channels // BLOCK
    tiles = 4
    spec = pl.BlockSpec((1, rows, tiles * BLOCK), lambda i: (0, 0, i))
    shape = jax.ShapeDtypeStruct(a.shape, a.dtype)
    return pl.pallas_call(
        functools.partial(post_kernel, tiles),
        grid=(pieces // tiles,),
        in_specs=[
            pl.BlockSpec((tiles, BLOCK, rows), lambda i: (i, 0, 0)),
            spec,
            spec,
        ],
        out_specs=[spec, spec],
        out_shape=[shape, shape],
        compiler_params=params(),
        cost_estimate=pl.CostEstimate(
            flops=2 * a.size, bytes_accessed=10 * a.size, transcendentals=0
        ),
    )(r, a, b)


def taps_kernel(sequences, taps_ref, lag_ref, out_ref):
    taps = taps_ref[...]
    length = taps.shape[1]
    root = jnp.sqrt(jnp.mean(taps * taps, axis=1, keepdims=True) + EPSILON)
    scale = 1.0 / (math.sqrt(length) * root)
    mean = lag_ref[...] / sequences
    projection = jnp.sum(mean * taps, axis=1, keepdims=True)
    out_ref[...] = scale * mean - taps * (scale * scale * scale) * projection


def taps_grad_of(taps, lag_total, sequences):
    return pl.pallas_call(
        functools.partial(taps_kernel, sequences),
        out_shape=jax.ShapeDtypeStruct(taps.shape, jnp.float32),
        compiler_params=params(),
    )(taps, lag_total)


def exchange(tiles):
    return lax.all_to_all(tiles, "ctx", split_axis=0, concat_axis=0, tiled=True)


def sum_over_dp(x):
    size = lax.axis_size("dp")
    step = 1
    while step < size:
        x = x + lax.ppermute(x, "dp", [(i, i ^ step) for i in range(size)])
        step *= 2
    return x


def shards(output_gate_input, key_input, value_input, upstream, filter_taps, order):
    groups = filter_taps.shape[0]
    product = exchange(pre(key_input, value_input))
    weighted = exchange(pre(upstream, output_gate_input))
    strip = strips(filter_taps)
    mixing = exchange(conv(order, product, strip, False))
    lag_sums = lag_sums_of(order, product, weighted, groups)
    returned = exchange(conv(order, weighted, strip, True))
    lag_total = sum_over_dp(lag_sums)
    mixed_out, gate_grad = post(mixing, output_gate_input, upstream)
    key_grad, value_grad = post(returned, value_input, key_input)
    taps_grad = taps_grad_of(filter_taps, lag_total, lax.axis_size("dp"))
    return mixed_out, gate_grad, key_grad, value_grad, taps_grad


def solution(mesh):
    rows = P("dp", "ctx", None)
    return jax.shard_map(
        shards,
        mesh=mesh,
        in_specs=(rows, rows, rows, rows, P("ctx", None), P()),
        out_specs=(rows, rows, rows, rows, P("ctx", None)),
        check_vma=False,
    )
```

```python
import functools
import math

import jax
import jax.numpy as jnp
from jax import lax
from jax.experimental import pallas as pl
from jax.experimental.pallas import tpu as pltpu
from jax.sharding import PartitionSpec as P

EPSILON = 1e-06
BLOCK = 128
GROUP = 16
MIB = 1024 * 1024
SPAN = 4

NN = (((1,), (0,)), ((), ()))
NT = (((1,), (1,)), ((), ()))
TN = (((0,), (0,)), ((), ()))


def dot(a, b, dims):
    return lax.dot_general(a, b, dims, preferred_element_type=jnp.float32)


def params(mib=60):
    return pltpu.CompilerParams(vmem_limit_bytes=mib * MIB)


def product_of(a, b):
    return a * b


def pre_kernel(tiles, a_ref, b_ref, out_ref):
    for i in range(tiles):
        cols = slice(i * BLOCK, (i + 1) * BLOCK)
        out_ref[i] = product_of(a_ref[0, :, cols], b_ref[0, :, cols]).T


def pre(a, b):
    _, rows, channels = a.shape
    pieces = channels // BLOCK
    tiles = 4
    spec = pl.BlockSpec((1, rows, tiles * BLOCK), lambda i: (0, 0, i))
    return pl.pallas_call(
        functools.partial(pre_kernel, tiles),
        grid=(pieces // tiles,),
        in_specs=[spec, spec],
        out_specs=pl.BlockSpec((tiles, BLOCK, rows), lambda i: (i, 0, 0)),
        out_shape=jax.ShapeDtypeStruct((pieces, BLOCK, rows), jnp.bfloat16),
        compiler_params=params(),
        cost_estimate=pl.CostEstimate(
            flops=a.size, bytes_accessed=6 * a.size, transcendentals=0
        ),
    )(a, b)


def strip_kernel(taps_ref, out_ref):
    g = pl.program_id(0)
    taps = taps_ref[pl.ds(g, 1), :]
    length = taps.shape[1]
    root = jnp.sqrt(jnp.mean(taps * taps, axis=1, keepdims=True) + EPSILON)
    row = taps * (1.0 / (math.sqrt(length) * root))
    width = length + BLOCK
    cur = jnp.concatenate([jnp.zeros((1, BLOCK), jnp.float32), row], axis=1)
    cur = jnp.broadcast_to(cur, (16, width))
    line = lax.broadcasted_iota(jnp.int32, (16, width), 0)
    for step in (1, 2, 4, 8):
        cur = jnp.where((line & step) != 0, pltpu.roll(cur, step, 1), cur)
    for q in range(BLOCK // 16):
        if q:
            cur = pltpu.roll(cur, 16, 1)
        out_ref[0, 16 * q : 16 * (q + 1), :] = cur.astype(jnp.bfloat16)
    out_ref[0, :, :BLOCK] = jnp.zeros((BLOCK, BLOCK), jnp.bfloat16)


def pre_strip_kernel(tiles, a_ref, b_ref, taps_ref, out_ref, strip_ref):
    pre_kernel(tiles, a_ref, b_ref, out_ref)
    strip_kernel(taps_ref, strip_ref)


def pre_and_strips(a, b, taps):
    _, rows, channels = a.shape
    pieces = channels // BLOCK
    groups, length = taps.shape
    tiles = pieces // groups
    width = length + BLOCK
    spec = pl.BlockSpec((1, rows, tiles * BLOCK), lambda i: (0, 0, i))
    return pl.pallas_call(
        functools.partial(pre_strip_kernel, tiles),
        grid=(groups,),
        in_specs=[spec, spec, pl.BlockSpec((groups, length), lambda i: (0, 0))],
        out_specs=[
            pl.BlockSpec((tiles, BLOCK, rows), lambda i: (i, 0, 0)),
            pl.BlockSpec((1, BLOCK, width), lambda i: (i, 0, 0)),
        ],
        out_shape=[
            jax.ShapeDtypeStruct((pieces, BLOCK, rows), jnp.bfloat16),
            jax.ShapeDtypeStruct((groups, BLOCK, width), jnp.bfloat16),
        ],
        compiler_params=params(),
        cost_estimate=pl.CostEstimate(
            flops=4 * groups * BLOCK * width,
            bytes_accessed=2 * groups * BLOCK * width + 6 * a.size,
            transcendentals=0,
        ),
    )(a, b, taps)


def rows_of(block):
    return pl.ds(pl.multiple_of(GROUP * block, GROUP), GROUP)


def conv_kernel(backward, order_ref, x_ref, strip_ref, out_ref, xs, acc):
    pieces = x_ref.shape[0]
    rows = acc.shape[1]
    spare = GROUP * (SPAN - 1)
    first = 0 if backward else SPAN - 1
    if backward:
        xs[:, rows : rows + spare, :] = jnp.zeros((2, spare, BLOCK), jnp.bfloat16)
    else:
        xs[:, :spare, :] = jnp.zeros((2, spare, BLOCK), jnp.bfloat16)
    for d in range(pieces):
        b = order_ref[d]
        xs[b % 2, rows_of(b // 2 + first), :] = x_ref[d]
    wide = 2 * BLOCK
    for lag in range(0, rows // GROUP, SPAN):
        depth = rows - GROUP * lag
        at = BLOCK + wide * lag
        lefts, weights = [], []
        for k in range(SPAN):
            start = GROUP * (lag + k) if backward else GROUP * (SPAN - 1 - k)
            lefts += [xs[0, start : start + depth, :], xs[1, start : start + depth, :]]
            weights += [
                strip_ref[0, :, at + wide * k : at + wide * (k + 1)],
                strip_ref[0, :, at + wide * k - BLOCK : at + wide * k + BLOCK],
            ]
        left = jnp.concatenate(lefts, axis=1)
        if backward:
            weights = [
                strip_ref[0, :, at : at + wide * SPAN],
                strip_ref[0, :, at - BLOCK : at - BLOCK + wide * SPAN],
            ]
        part = dot(left, jnp.concatenate(weights, axis=0), NT if backward else NN)
        if lag == 0:
            acc[0] = part[:, :BLOCK]
            acc[1] = part[:, BLOCK:]
        else:
            target = slice(0, depth) if backward else slice(rows - depth, rows)
            acc[0, target, :] += part[:, :BLOCK]
            acc[1, target, :] += part[:, BLOCK:]
    for d in range(pieces):
        b = order_ref[d]
        out_ref[d] = acc[b % 2, rows_of(b // 2), :].astype(jnp.bfloat16)


def conv_scratch(rows):
    return [
        pltpu.VMEM((2, rows + GROUP * (SPAN - 1), BLOCK), jnp.bfloat16),
        pltpu.VMEM((2, rows, BLOCK), jnp.float32),
    ]


def forward(order, x, strip):
    pieces = x.shape[0]
    groups, _, width = strip.shape
    rows = GROUP * pieces // 2
    spec = pl.BlockSpec((pieces, GROUP, BLOCK), lambda g, order: (0, g, 0))
    return pl.pallas_call(
        functools.partial(conv_kernel, False),
        grid_spec=pltpu.PrefetchScalarGridSpec(
            num_scalar_prefetch=1,
            grid=(groups,),
            in_specs=[
                spec,
                pl.BlockSpec((1, BLOCK, width), lambda g, order: (g, 0, 0)),
            ],
            out_specs=spec,
            scratch_shapes=conv_scratch(rows),
        ),
        out_shape=jax.ShapeDtypeStruct(x.shape, jnp.bfloat16),
        compiler_params=params(),
        cost_estimate=pl.CostEstimate(
            flops=groups * rows * rows * 16 * BLOCK,
            bytes_accessed=4 * x.size + 2 * strip.size,
            transcendentals=0,
        ),
    )(order, x, strip)


def lag_kernel(order_ref, x_ref, w_ref, out_ref, xs, ws, squares):
    pieces = x_ref.shape[0]
    total = GROUP * pieces
    for d in range(pieces):
        rows = rows_of(order_ref[d])
        xs[rows, :] = x_ref[d]
        ws[rows, :] = w_ref[d]
    ws[total:, :] = jnp.zeros((BLOCK, BLOCK), jnp.bfloat16)
    x_turned = xs[...].T
    for lag in range(0, pieces, 2):
        depth = total - GROUP * lag // BLOCK * BLOCK
        start = GROUP * lag
        if start + GROUP + depth > total + BLOCK:
            raise ValueError("spare rows")
        right = jnp.concatenate(
            [ws[start : start + depth, :], ws[start + GROUP : start + GROUP + depth, :]],
            axis=1,
        )
        squares[:, lag * BLOCK : (lag + 2) * BLOCK] = dot(x_turned[:, :depth], right, NN)
    row = lax.broadcasted_iota(jnp.int32, (BLOCK, BLOCK), 0)
    col = lax.broadcasted_iota(jnp.int32, (BLOCK, BLOCK), 1)
    squares[:, :BLOCK] = jnp.where(col >= row, squares[:, :BLOCK], 0.0)
    width = squares.shape[1]
    cur = squares[BLOCK - 8 :, :]
    for q in range(BLOCK // 8 - 2, -1, -1):
        cur = pltpu.roll(cur, width - 8, 1) + squares[8 * q : 8 * (q + 1), :]
    line = lax.broadcasted_iota(jnp.int32, (8, width), 0)
    for step in (1, 2, 4):
        cur = jnp.where((line & step) != 0, pltpu.roll(cur, width - step, 1), cur)
    out_ref[pl.ds(pl.program_id(0), 1), :] = jnp.sum(cur, axis=0, keepdims=True)


def back_kernel(
    order_ref, x_ref, w_ref, strip_ref, out_ref, lag_ref, pairs, acc, xs, ws, squares
):
    conv_kernel(True, order_ref, w_ref, strip_ref, out_ref, pairs, acc)
    lag_kernel(order_ref, x_ref, w_ref, lag_ref, xs, ws, squares)


def back(order, x, w, strip):
    pieces = x.shape[0]
    groups, _, width = strip.shape
    length = pieces * BLOCK
    rows = GROUP * pieces
    spec = pl.BlockSpec((pieces, GROUP, BLOCK), lambda g, order: (0, g, 0))
    return pl.pallas_call(
        back_kernel,
        grid_spec=pltpu.PrefetchScalarGridSpec(
            num_scalar_prefetch=1,
            grid=(groups,),
            in_specs=[
                spec,
                spec,
                pl.BlockSpec((1, BLOCK, width), lambda g, order: (g, 0, 0)),
            ],
            out_specs=[spec, pl.BlockSpec((groups, length), lambda g, order: (0, 0))],
            scratch_shapes=conv_scratch(rows // 2)
            + [
                pltpu.VMEM((rows, BLOCK), jnp.bfloat16),
                pltpu.VMEM((rows + BLOCK, BLOCK), jnp.bfloat16),
                pltpu.VMEM((BLOCK, length), jnp.float32),
            ],
        ),
        out_shape=[
            jax.ShapeDtypeStruct(x.shape, jnp.bfloat16),
            jax.ShapeDtypeStruct((groups, length), jnp.float32),
        ],
        compiler_params=params(),
        cost_estimate=pl.CostEstimate(
            flops=2 * groups * rows * BLOCK * length,
            bytes_accessed=6 * x.size + 2 * strip.size,
            transcendentals=0,
        ),
    )(order, x, w, strip)


def post_kernel(tiles, r_ref, a_ref, b_ref, out_a_ref, out_b_ref):
    for i in range(tiles):
        cols = slice(i * BLOCK, (i + 1) * BLOCK)
        turned = r_ref[i].T
        out_a_ref[0, :, cols] = product_of(a_ref[0, :, cols], turned)
        out_b_ref[0, :, cols] = product_of(b_ref[0, :, cols], turned)


def post(r, a, b):
    _, rows, channels = a.shape
    pieces = channels // BLOCK
    tiles = 4
    spec = pl.BlockSpec((1, rows, tiles * BLOCK), lambda i: (0, 0, i))
    shape = jax.ShapeDtypeStruct(a.shape, a.dtype)
    return pl.pallas_call(
        functools.partial(post_kernel, tiles),
        grid=(pieces // tiles,),
        in_specs=[
            pl.BlockSpec((tiles, BLOCK, rows), lambda i: (i, 0, 0)),
            spec,
            spec,
        ],
        out_specs=[spec, spec],
        out_shape=[shape, shape],
        compiler_params=params(32),
        cost_estimate=pl.CostEstimate(
            flops=2 * a.size, bytes_accessed=10 * a.size, transcendentals=0
        ),
    )(r, a, b)


def taps_kernel(sequences, taps_ref, lag_ref, out_ref):
    taps = taps_ref[...]
    length = taps.shape[1]
    root = jnp.sqrt(jnp.mean(taps * taps, axis=1, keepdims=True) + EPSILON)
    scale = 1.0 / (math.sqrt(length) * root)
    mean = lag_ref[...] / sequences
    projection = jnp.sum(mean * taps, axis=1, keepdims=True)
    out_ref[...] = scale * mean - taps * (scale * scale * scale) * projection


def taps_grad_of(taps, lag_total, sequences):
    return pl.pallas_call(
        functools.partial(taps_kernel, sequences),
        out_shape=jax.ShapeDtypeStruct(taps.shape, jnp.float32),
        compiler_params=params(),
    )(taps, lag_total)


def exchange(tiles):
    return lax.all_to_all(tiles, "ctx", split_axis=0, concat_axis=0, tiled=True)


def sum_over_dp(x):
    size = lax.axis_size("dp")
    step = 1
    while step < size:
        x = x + lax.ppermute(x, "dp", [(i, i ^ step) for i in range(size)])
        step *= 2
    return x


def shards(output_gate_input, key_input, value_input, upstream, filter_taps, order):
    product_tiles = pre(key_input, value_input)
    product = exchange(product_tiles)
    weighted_tiles, strip = pre_and_strips(upstream, output_gate_input, filter_taps)
    weighted = exchange(weighted_tiles)
    mixing = exchange(forward(order, product, strip))
    returned_tiles, lag_sums = back(order, product, weighted, strip)
    returned = exchange(returned_tiles)
    lag_total = sum_over_dp(lag_sums)
    mixed_out, gate_grad = post(mixing, output_gate_input, upstream)
    taps_grad = taps_grad_of(filter_taps, lag_total, lax.axis_size("dp"))
    key_grad, value_grad = post(returned, value_input, key_input)
    return mixed_out, gate_grad, key_grad, value_grad, taps_grad


def solution(mesh):
    rows = P("dp", "ctx", None)
    return jax.shard_map(
        shards,
        mesh=mesh,
        in_specs=(rows, rows, rows, rows, P("ctx", None), P()),
        out_specs=(rows, rows, rows, rows, P("ctx", None)),
        check_vma=False,
    )
```

```python
import functools
import math

import jax
import jax.numpy as jnp
from jax import lax
from jax.experimental import pallas as pl
from jax.experimental.pallas import tpu as pltpu
from jax.sharding import PartitionSpec as P

EPSILON = 1e-06
BLOCK = 128
GROUP = 16
MIB = 1024 * 1024
SPAN = 4
CHUNKS = 4

NN = (((1,), (0,)), ((), ()))
NT = (((1,), (1,)), ((), ()))
TN = (((0,), (0,)), ((), ()))


def dot(a, b, dims):
    return lax.dot_general(a, b, dims, preferred_element_type=jnp.float32)


def params(mib=60):
    return pltpu.CompilerParams(vmem_limit_bytes=mib * MIB)


def product_of(a, b):
    return a * b


def copies(source, target, sems, chunks):
    step = source.shape[-1] // chunks
    made = []
    for i in range(chunks):
        cols = pl.ds(i * step, step)
        made.append(
            pltpu.make_async_copy(source.at[0, :, cols], target.at[0, :, cols], sems.at[i])
        )
    return made


def tile_copies(source, target, sems, chunks):
    step = source.shape[0] // chunks
    made = []
    for i in range(chunks):
        part = pl.ds(i * step, step)
        made.append(pltpu.make_async_copy(source.at[part], target.at[part], sems.at[i]))
    return made


def pre_kernel(a_hbm, b_hbm, out_hbm, a, b, out, a_sem, b_sem, out_sem):
    into = list(
        zip(copies(a_hbm, a, a_sem, CHUNKS), copies(b_hbm, b, b_sem, CHUNKS), strict=True)
    )
    back = tile_copies(out, out_hbm, out_sem, CHUNKS)
    for pair in into:
        for copy in pair:
            copy.start()
    tiles = out.shape[0] // CHUNKS
    for i in range(CHUNKS):
        for copy in into[i]:
            copy.wait()
        for t in range(i * tiles, (i + 1) * tiles):
            cols = slice(t * BLOCK, (t + 1) * BLOCK)
            out[t] = product_of(a[0, :, cols], b[0, :, cols]).T
        back[i].start()
    for copy in back:
        copy.wait()


def pre(a, b):
    _, rows, channels = a.shape
    tiles = (channels // BLOCK, BLOCK, rows)
    anywhere = pl.BlockSpec(memory_space=pl.ANY)
    return pl.pallas_call(
        pre_kernel,
        in_specs=[anywhere, anywhere],
        out_specs=anywhere,
        out_shape=jax.ShapeDtypeStruct(tiles, jnp.bfloat16),
        scratch_shapes=[
            pltpu.VMEM(a.shape, jnp.bfloat16),
            pltpu.VMEM(b.shape, jnp.bfloat16),
            pltpu.VMEM(tiles, jnp.bfloat16),
        ]
        + [pltpu.SemaphoreType.DMA((CHUNKS,))] * 3,
        compiler_params=params(),
        cost_estimate=pl.CostEstimate(
            flops=a.size, bytes_accessed=6 * a.size, transcendentals=0
        ),
    )(a, b)


def strip_kernel(taps_ref, out_ref):
    g = pl.program_id(0)
    taps = taps_ref[pl.ds(g, 1), :]
    length = taps.shape[1]
    root = jnp.sqrt(jnp.mean(taps * taps, axis=1, keepdims=True) + EPSILON)
    row = taps * (1.0 / (math.sqrt(length) * root))
    width = length + BLOCK
    cur = jnp.concatenate([jnp.zeros((1, BLOCK), jnp.float32), row], axis=1)
    cur = jnp.broadcast_to(cur, (16, width))
    line = lax.broadcasted_iota(jnp.int32, (16, width), 0)
    for step in (1, 2, 4, 8):
        cur = jnp.where((line & step) != 0, pltpu.roll(cur, step, 1), cur)
    for q in range(BLOCK // 16):
        if q:
            cur = pltpu.roll(cur, 16, 1)
        out_ref[0, 16 * q : 16 * (q + 1), :] = cur.astype(jnp.bfloat16)
    out_ref[0, :, :BLOCK] = jnp.zeros((BLOCK, BLOCK), jnp.bfloat16)


def pre_strip_kernel(tiles, a_ref, b_ref, taps_ref, out_ref, strip_ref):
    for i in range(tiles):
        cols = slice(i * BLOCK, (i + 1) * BLOCK)
        out_ref[i] = product_of(a_ref[0, :, cols], b_ref[0, :, cols]).T
    strip_kernel(taps_ref, strip_ref)


def pre_and_strips(a, b, taps):
    _, rows, channels = a.shape
    pieces = channels // BLOCK
    groups, length = taps.shape
    tiles = pieces // groups
    width = length + BLOCK
    spec = pl.BlockSpec((1, rows, tiles * BLOCK), lambda i: (0, 0, i))
    return pl.pallas_call(
        functools.partial(pre_strip_kernel, tiles),
        grid=(groups,),
        in_specs=[spec, spec, pl.BlockSpec((groups, length), lambda i: (0, 0))],
        out_specs=[
            pl.BlockSpec((tiles, BLOCK, rows), lambda i: (i, 0, 0)),
            pl.BlockSpec((1, BLOCK, width), lambda i: (i, 0, 0)),
        ],
        out_shape=[
            jax.ShapeDtypeStruct((pieces, BLOCK, rows), jnp.bfloat16),
            jax.ShapeDtypeStruct((groups, BLOCK, width), jnp.bfloat16),
        ],
        compiler_params=params(),
        cost_estimate=pl.CostEstimate(
            flops=4 * groups * BLOCK * width,
            bytes_accessed=2 * groups * BLOCK * width + 6 * a.size,
            transcendentals=0,
        ),
    )(a, b, taps)


def rows_of(block):
    return pl.ds(pl.multiple_of(GROUP * block, GROUP), GROUP)


def conv_kernel(backward, order_ref, x_ref, strip_ref, out_ref, xs, acc):
    pieces = x_ref.shape[0]
    rows = acc.shape[1]
    spare = GROUP * (SPAN - 1)
    first = 0 if backward else SPAN - 1
    if backward:
        xs[:, rows : rows + spare, :] = jnp.zeros((2, spare, BLOCK), jnp.bfloat16)
    else:
        xs[:, :spare, :] = jnp.zeros((2, spare, BLOCK), jnp.bfloat16)
    for d in range(pieces):
        b = order_ref[d]
        xs[b % 2, rows_of(b // 2 + first), :] = x_ref[d, rows_of(pl.program_id(0)), :]
    wide = 2 * BLOCK
    for lag in range(0, rows // GROUP, SPAN):
        depth = rows - GROUP * lag
        at = BLOCK + wide * lag
        lefts, weights = [], []
        for k in range(SPAN):
            start = GROUP * (lag + k) if backward else GROUP * (SPAN - 1 - k)
            lefts += [xs[0, start : start + depth, :], xs[1, start : start + depth, :]]
            weights += [
                strip_ref[0, :, at + wide * k : at + wide * (k + 1)],
                strip_ref[0, :, at + wide * k - BLOCK : at + wide * k + BLOCK],
            ]
        left = jnp.concatenate(lefts, axis=1)
        if backward:
            weights = [
                strip_ref[0, :, at : at + wide * SPAN],
                strip_ref[0, :, at - BLOCK : at - BLOCK + wide * SPAN],
            ]
        part = dot(left, jnp.concatenate(weights, axis=0), NT if backward else NN)
        if lag == 0:
            acc[0] = part[:, :BLOCK]
            acc[1] = part[:, BLOCK:]
        else:
            target = slice(0, depth) if backward else slice(rows - depth, rows)
            acc[0, target, :] += part[:, :BLOCK]
            acc[1, target, :] += part[:, BLOCK:]
    for d in range(pieces):
        b = order_ref[d]
        out_ref[d] = acc[b % 2, rows_of(b // 2), :].astype(jnp.bfloat16)


def conv_scratch(rows):
    return [
        pltpu.VMEM((2, rows + GROUP * (SPAN - 1), BLOCK), jnp.bfloat16),
        pltpu.VMEM((2, rows, BLOCK), jnp.float32),
    ]


def forward(order, x, strip):
    pieces = x.shape[0]
    groups, _, width = strip.shape
    rows = GROUP * pieces // 2
    spec = pl.BlockSpec((pieces, GROUP, BLOCK), lambda g, order: (0, g, 0))
    return pl.pallas_call(
        functools.partial(conv_kernel, False),
        grid_spec=pltpu.PrefetchScalarGridSpec(
            num_scalar_prefetch=1,
            grid=(groups,),
            in_specs=[
                pl.BlockSpec(x.shape, lambda g, order: (0, 0, 0)),
                pl.BlockSpec((1, BLOCK, width), lambda g, order: (g, 0, 0)),
            ],
            out_specs=spec,
            scratch_shapes=conv_scratch(rows),
        ),
        out_shape=jax.ShapeDtypeStruct(x.shape, jnp.bfloat16),
        compiler_params=params(),
        cost_estimate=pl.CostEstimate(
            flops=groups * rows * rows * 16 * BLOCK,
            bytes_accessed=4 * x.size + 2 * strip.size,
            transcendentals=0,
        ),
    )(order, x, strip)


def lag_kernel(order_ref, x_ref, w_ref, out_ref, xs, ws, squares, sums):
    pieces = x_ref.shape[0]
    total = GROUP * pieces
    last = BLOCK - 1
    g = pl.program_id(0)
    for d in range(pieces):
        rows = rows_of(order_ref[d])
        xs[rows, :] = x_ref[d, rows_of(g), :]
        ws[rows, :] = w_ref[d, rows_of(g), :]
    ws[total:, :] = jnp.zeros((BLOCK, BLOCK), jnp.bfloat16)
    row = lax.broadcasted_iota(jnp.int32, (BLOCK, BLOCK), 0)
    col = lax.broadcasted_iota(jnp.int32, (BLOCK, BLOCK), 1)
    mirror = jnp.where(row + col == last, 1.0, 0.0).astype(jnp.bfloat16)
    x_turned = dot(mirror, xs[...], NT).astype(jnp.bfloat16)
    for lag in range(0, pieces, 2):
        depth = total - GROUP * lag // BLOCK * BLOCK
        start = GROUP * lag
        right = jnp.concatenate(
            [ws[start : start + depth, :], ws[start + GROUP : start + GROUP + depth, :]],
            axis=1,
        )
        squares[:, lag * BLOCK : (lag + 2) * BLOCK] = dot(x_turned[:, :depth], right, NN)
    squares[:, pieces * BLOCK :] = jnp.zeros((BLOCK, BLOCK), jnp.float32)
    step = 8
    for t in range(0, pieces, step):
        cols = slice(t * BLOCK, (t + step + 1) * BLOCK)
        added = None
        for q in range(BLOCK // 8):
            moved = pltpu.roll(squares[8 * q : 8 * q + 8, cols], 8 * q, 1, stride=1, stride_axis=0)
            added = moved if added is None else added + moved
        added = jnp.sum(added, axis=0, keepdims=True)
        skip = BLOCK if t else 0
        sums[pl.ds(g, 1), t * BLOCK + skip : (t + step + 1) * BLOCK] = added[:, skip:]

    @pl.when(g == pl.num_programs(0) - 1)
    def _():
        width = sums.shape[1]
        out_ref[...] = pltpu.roll(sums[...], width - last, 1)[:, : pieces * BLOCK]


def back_kernel(
    order_ref, x_ref, w_ref, strip_ref, out_ref, lag_ref, pairs, acc, xs, ws, squares, sums
):
    conv_kernel(True, order_ref, w_ref, strip_ref, out_ref, pairs, acc)
    lag_kernel(order_ref, x_ref, w_ref, lag_ref, xs, ws, squares, sums)


def back(order, x, w, strip):
    pieces = x.shape[0]
    groups, _, width = strip.shape
    length = pieces * BLOCK
    rows = GROUP * pieces
    spec = pl.BlockSpec((pieces, GROUP, BLOCK), lambda g, order: (0, g, 0))
    return pl.pallas_call(
        back_kernel,
        grid_spec=pltpu.PrefetchScalarGridSpec(
            num_scalar_prefetch=1,
            grid=(groups,),
            in_specs=[
                pl.BlockSpec(x.shape, lambda g, order: (0, 0, 0)),
                pl.BlockSpec(x.shape, lambda g, order: (0, 0, 0)),
                pl.BlockSpec((1, BLOCK, width), lambda g, order: (g, 0, 0)),
            ],
            out_specs=[spec, pl.BlockSpec((groups, length), lambda g, order: (0, 0))],
            scratch_shapes=conv_scratch(rows // 2)
            + [
                pltpu.VMEM((rows, BLOCK), jnp.bfloat16),
                pltpu.VMEM((rows + BLOCK, BLOCK), jnp.bfloat16),
                pltpu.VMEM((BLOCK, length + BLOCK), jnp.float32),
                pltpu.VMEM((groups, length + BLOCK), jnp.float32),
            ],
        ),
        out_shape=[
            jax.ShapeDtypeStruct(x.shape, jnp.bfloat16),
            jax.ShapeDtypeStruct((groups, length), jnp.float32),
        ],
        compiler_params=params(),
        cost_estimate=pl.CostEstimate(
            flops=2 * groups * rows * BLOCK * length,
            bytes_accessed=6 * x.size + 2 * strip.size,
            transcendentals=0,
        ),
    )(order, x, w, strip)


def post_kernel(
    r_hbm, a_hbm, b_hbm, x_hbm, y_hbm, r, a, b, x, y, r_sem, a_sem, b_sem, x_sem, y_sem
):
    into = list(
        zip(
            tile_copies(r_hbm, r, r_sem, CHUNKS),
            copies(a_hbm, a, a_sem, CHUNKS),
            copies(b_hbm, b, b_sem, CHUNKS),
            strict=True,
        )
    )
    back = list(
        zip(copies(x, x_hbm, x_sem, CHUNKS), copies(y, y_hbm, y_sem, CHUNKS), strict=True)
    )
    for group in into:
        for copy in group:
            copy.start()
    tiles = r.shape[0] // CHUNKS
    for i in range(CHUNKS):
        for copy in into[i]:
            copy.wait()
        for t in range(i * tiles, (i + 1) * tiles):
            cols = slice(t * BLOCK, (t + 1) * BLOCK)
            turned = r[t].T
            x[0, :, cols] = product_of(a[0, :, cols], turned)
            y[0, :, cols] = product_of(b[0, :, cols], turned)
        for copy in back[i]:
            copy.start()
    for group in back:
        for copy in group:
            copy.wait()


def post(r, a, b):
    anywhere = pl.BlockSpec(memory_space=pl.ANY)
    shape = jax.ShapeDtypeStruct(a.shape, a.dtype)
    return pl.pallas_call(
        post_kernel,
        in_specs=[anywhere] * 3,
        out_specs=[anywhere] * 2,
        out_shape=[shape, shape],
        scratch_shapes=[pltpu.VMEM(r.shape, r.dtype)]
        + [pltpu.VMEM(a.shape, a.dtype)] * 4
        + [pltpu.SemaphoreType.DMA((CHUNKS,))] * 5,
        compiler_params=params(),
        cost_estimate=pl.CostEstimate(
            flops=2 * a.size, bytes_accessed=10 * a.size, transcendentals=0
        ),
    )(r, a, b)


def taps_kernel(sequences, taps_ref, lag_ref, out_ref):
    taps = taps_ref[...]
    length = taps.shape[1]
    root = jnp.sqrt(jnp.mean(taps * taps, axis=1, keepdims=True) + EPSILON)
    scale = 1.0 / (math.sqrt(length) * root)
    mean = lag_ref[...] / sequences
    projection = jnp.sum(mean * taps, axis=1, keepdims=True)
    out_ref[...] = scale * mean - taps * (scale * scale * scale) * projection


def taps_grad_of(taps, lag_total, sequences):
    return pl.pallas_call(
        functools.partial(taps_kernel, sequences),
        out_shape=jax.ShapeDtypeStruct(taps.shape, jnp.float32),
        compiler_params=params(),
    )(taps, lag_total)


def exchange(tiles):
    return lax.all_to_all(tiles, "ctx", split_axis=0, concat_axis=0, tiled=True)


def sum_over_dp(x):
    size = lax.axis_size("dp")
    step = 1
    while step < size:
        x = x + lax.ppermute(x, "dp", [(i, i ^ step) for i in range(size)])
        step *= 2
    return x


def shards(output_gate_input, key_input, value_input, upstream, filter_taps, order):
    product_tiles = pre(key_input, value_input)
    product = exchange(product_tiles)
    weighted_tiles, strip = pre_and_strips(upstream, output_gate_input, filter_taps)
    weighted = exchange(weighted_tiles)
    mixing = exchange(forward(order, product, strip))
    returned_tiles, lag_sums = back(order, product, weighted, strip)
    returned = exchange(returned_tiles)
    lag_total = sum_over_dp(lag_sums)
    mixed_out, gate_grad = post(mixing, output_gate_input, upstream)
    taps_grad = taps_grad_of(filter_taps, lag_total, lax.axis_size("dp"))
    key_grad, value_grad = post(returned, value_input, key_input)
    return mixed_out, gate_grad, key_grad, value_grad, taps_grad


def solution(mesh):
    rows = P("dp", "ctx", None)
    return jax.shard_map(
        shards,
        mesh=mesh,
        in_specs=(rows, rows, rows, rows, P("ctx", None), P()),
        out_specs=(rows, rows, rows, rows, P("ctx", None)),
        check_vma=False,
    )
```

```python
import functools
import math

import jax
import jax.numpy as jnp
from jax import lax
from jax.experimental import pallas as pl
from jax.experimental.pallas import tpu as pltpu
from jax.sharding import PartitionSpec as P

EPSILON = 1e-06
BLOCK = 128
GROUP = 16
MIB = 1024 * 1024
SPAN = 4
CHUNKS = 4

SHORT = pl.CostEstimate(flops=1000, bytes_accessed=1000, transcendentals=0)
LONG = pl.CostEstimate(flops=10**10, bytes_accessed=1000, transcendentals=0)

NN = (((1,), (0,)), ((), ()))
NT = (((1,), (1,)), ((), ()))
TN = (((0,), (0,)), ((), ()))


def dot(a, b, dims):
    return lax.dot_general(a, b, dims, preferred_element_type=jnp.float32)


def params(mib=60):
    return pltpu.CompilerParams(vmem_limit_bytes=mib * MIB)


def product_of(a, b):
    return a * b


def copies(source, target, sems, chunks):
    step = source.shape[-1] // chunks
    made = []
    for i in range(chunks):
        cols = pl.ds(i * step, step)
        made.append(
            pltpu.make_async_copy(source.at[0, :, cols], target.at[0, :, cols], sems.at[i])
        )
    return made


def tile_copies(source, target, sems, chunks):
    step = source.shape[0] // chunks
    made = []
    for i in range(chunks):
        part = pl.ds(i * step, step)
        made.append(pltpu.make_async_copy(source.at[part], target.at[part], sems.at[i]))
    return made


def pre_kernel(a_hbm, b_hbm, out_hbm, a, b, out, a_sem, b_sem, out_sem):
    into = list(
        zip(copies(a_hbm, a, a_sem, CHUNKS), copies(b_hbm, b, b_sem, CHUNKS), strict=True)
    )
    back = tile_copies(out, out_hbm, out_sem, CHUNKS)
    for pair in into:
        for copy in pair:
            copy.start()
    tiles = out.shape[0] // CHUNKS
    for i in range(CHUNKS):
        for copy in into[i]:
            copy.wait()
        for t in range(i * tiles, (i + 1) * tiles):
            cols = slice(t * BLOCK, (t + 1) * BLOCK)
            out[t] = product_of(a[0, :, cols], b[0, :, cols]).T
        back[i].start()
    for copy in back:
        copy.wait()


def pre(a, b):
    _, rows, channels = a.shape
    tiles = (channels // BLOCK, BLOCK, rows)
    anywhere = pl.BlockSpec(memory_space=pl.ANY)
    return pl.pallas_call(
        pre_kernel,
        in_specs=[anywhere, anywhere],
        out_specs=anywhere,
        out_shape=jax.ShapeDtypeStruct(tiles, jnp.bfloat16),
        scratch_shapes=[
            pltpu.VMEM(a.shape, jnp.bfloat16),
            pltpu.VMEM(b.shape, jnp.bfloat16),
            pltpu.VMEM(tiles, jnp.bfloat16),
        ]
        + [pltpu.SemaphoreType.DMA((CHUNKS,))] * 3,
        compiler_params=params(),
        cost_estimate=pl.CostEstimate(
            flops=a.size, bytes_accessed=6 * a.size, transcendentals=0
        ),
    )(a, b)


def strip_kernel(taps_ref, out_ref):
    g = pl.program_id(0)
    taps = taps_ref[pl.ds(g, 1), :]
    length = taps.shape[1]
    root = jnp.sqrt(jnp.mean(taps * taps, axis=1, keepdims=True) + EPSILON)
    row = taps * (1.0 / (math.sqrt(length) * root))
    width = length + BLOCK
    cur = jnp.concatenate([jnp.zeros((1, BLOCK), jnp.float32), row], axis=1)
    cur = jnp.broadcast_to(cur, (16, width))
    line = lax.broadcasted_iota(jnp.int32, (16, width), 0)
    for step in (1, 2, 4, 8):
        cur = jnp.where((line & step) != 0, pltpu.roll(cur, step, 1), cur)
    for q in range(BLOCK // 16):
        if q:
            cur = pltpu.roll(cur, 16, 1)
        out_ref[0, 16 * q : 16 * (q + 1), :] = cur.astype(jnp.bfloat16)
    out_ref[0, :, :BLOCK] = jnp.zeros((BLOCK, BLOCK), jnp.bfloat16)


def pre_strip_kernel(tiles, a_ref, b_ref, taps_ref, out_ref, strip_ref):
    for i in range(tiles):
        cols = slice(i * BLOCK, (i + 1) * BLOCK)
        out_ref[i] = product_of(a_ref[0, :, cols], b_ref[0, :, cols]).T
    strip_kernel(taps_ref, strip_ref)


def pre_and_strips(a, b, taps):
    _, rows, channels = a.shape
    pieces = channels // BLOCK
    groups, length = taps.shape
    tiles = pieces // groups
    width = length + BLOCK
    spec = pl.BlockSpec((1, rows, tiles * BLOCK), lambda i: (0, 0, i))
    return pl.pallas_call(
        functools.partial(pre_strip_kernel, tiles),
        grid=(groups,),
        in_specs=[spec, spec, pl.BlockSpec((groups, length), lambda i: (0, 0))],
        out_specs=[
            pl.BlockSpec((tiles, BLOCK, rows), lambda i: (i, 0, 0)),
            pl.BlockSpec((1, BLOCK, width), lambda i: (i, 0, 0)),
        ],
        out_shape=[
            jax.ShapeDtypeStruct((pieces, BLOCK, rows), jnp.bfloat16),
            jax.ShapeDtypeStruct((groups, BLOCK, width), jnp.bfloat16),
        ],
        compiler_params=params(),
        cost_estimate=pl.CostEstimate(
            flops=4 * groups * BLOCK * width,
            bytes_accessed=2 * groups * BLOCK * width + 6 * a.size,
            transcendentals=0,
        ),
    )(a, b, taps)


def rows_of(block):
    return pl.ds(pl.multiple_of(GROUP * block, GROUP), GROUP)


def conv_kernel(backward, order_ref, x_ref, strip_ref, out_ref, xs, acc):
    pieces = x_ref.shape[0]
    rows = acc.shape[1]
    spare = GROUP * (SPAN - 1)
    first = 0 if backward else SPAN - 1
    if backward:
        xs[:, rows : rows + spare, :] = jnp.zeros((2, spare, BLOCK), jnp.bfloat16)
    else:
        xs[:, :spare, :] = jnp.zeros((2, spare, BLOCK), jnp.bfloat16)
    for d in range(pieces):
        b = order_ref[d]
        xs[b % 2, rows_of(b // 2 + first), :] = x_ref[d, rows_of(pl.program_id(0)), :]
    wide = 2 * BLOCK
    for lag in range(0, rows // GROUP, SPAN):
        depth = rows - GROUP * lag
        at = BLOCK + wide * lag
        lefts, weights = [], []
        for k in range(SPAN):
            start = GROUP * (lag + k) if backward else GROUP * (SPAN - 1 - k)
            lefts += [xs[0, start : start + depth, :], xs[1, start : start + depth, :]]
            weights += [
                strip_ref[0, :, at + wide * k : at + wide * (k + 1)],
                strip_ref[0, :, at + wide * k - BLOCK : at + wide * k + BLOCK],
            ]
        left = jnp.concatenate(lefts, axis=1)
        if backward:
            weights = [
                strip_ref[0, :, at : at + wide * SPAN],
                strip_ref[0, :, at - BLOCK : at - BLOCK + wide * SPAN],
            ]
        part = dot(left, jnp.concatenate(weights, axis=0), NT if backward else NN)
        if lag == 0:
            acc[0] = part[:, :BLOCK]
            acc[1] = part[:, BLOCK:]
        else:
            target = slice(0, depth) if backward else slice(rows - depth, rows)
            acc[0, target, :] += part[:, :BLOCK]
            acc[1, target, :] += part[:, BLOCK:]
    for d in range(pieces):
        b = order_ref[d]
        out_ref[d] = acc[b % 2, rows_of(b // 2), :].astype(jnp.bfloat16)


def conv_scratch(rows):
    return [
        pltpu.VMEM((2, rows + GROUP * (SPAN - 1), BLOCK), jnp.bfloat16),
        pltpu.VMEM((2, rows, BLOCK), jnp.float32),
    ]


def conv(order, x, strip, backward):
    pieces = x.shape[0]
    groups, _, width = strip.shape
    rows = GROUP * pieces // 2
    spec = pl.BlockSpec((pieces, GROUP, BLOCK), lambda g, order: (0, g, 0))
    return pl.pallas_call(
        functools.partial(conv_kernel, backward),
        grid_spec=pltpu.PrefetchScalarGridSpec(
            num_scalar_prefetch=1,
            grid=(groups,),
            in_specs=[
                pl.BlockSpec(x.shape, lambda g, order: (0, 0, 0)),
                pl.BlockSpec((1, BLOCK, width), lambda g, order: (g, 0, 0)),
            ],
            out_specs=spec,
            scratch_shapes=conv_scratch(rows),
        ),
        out_shape=jax.ShapeDtypeStruct(x.shape, jnp.bfloat16),
        compiler_params=params(),
        cost_estimate=LONG if backward else SHORT,
    )(order, x, strip)


def lag_kernel(order_ref, x_ref, w_ref, out_ref, xs, ws, squares, sums):
    pieces = x_ref.shape[0]
    total = GROUP * pieces
    last = BLOCK - 1
    g = pl.program_id(0)
    for d in range(pieces):
        rows = rows_of(order_ref[d])
        xs[rows, :] = x_ref[d, rows_of(g), :]
        ws[rows, :] = w_ref[d, rows_of(g), :]
    ws[total:, :] = jnp.zeros((BLOCK, BLOCK), jnp.bfloat16)
    row = lax.broadcasted_iota(jnp.int32, (BLOCK, BLOCK), 0)
    col = lax.broadcasted_iota(jnp.int32, (BLOCK, BLOCK), 1)
    mirror = jnp.where(row + col == last, 1.0, 0.0).astype(jnp.bfloat16)
    x_turned = dot(mirror, xs[...], NT).astype(jnp.bfloat16)
    for lag in range(0, pieces, 2):
        depth = total - GROUP * lag // BLOCK * BLOCK
        start = GROUP * lag
        right = jnp.concatenate(
            [ws[start : start + depth, :], ws[start + GROUP : start + GROUP + depth, :]],
            axis=1,
        )
        squares[:, lag * BLOCK : (lag + 2) * BLOCK] = dot(x_turned[:, :depth], right, NN)
    squares[:, pieces * BLOCK :] = jnp.zeros((BLOCK, BLOCK), jnp.float32)
    step = 8
    for t in range(0, pieces, step):
        cols = slice(t * BLOCK, (t + step + 1) * BLOCK)
        added = None
        for q in range(BLOCK // 8):
            moved = pltpu.roll(squares[8 * q : 8 * q + 8, cols], 8 * q, 1, stride=1, stride_axis=0)
            added = moved if added is None else added + moved
        added = jnp.sum(added, axis=0, keepdims=True)
        skip = BLOCK if t else 0
        sums[pl.ds(g, 1), t * BLOCK + skip : (t + step + 1) * BLOCK] = added[:, skip:]

    @pl.when(g == pl.num_programs(0) - 1)
    def _():
        width = sums.shape[1]
        out_ref[...] = pltpu.roll(sums[...], width - last, 1)[:, : pieces * BLOCK]


def lag_sums_of(order, x, w, groups):
    pieces = x.shape[0]
    length = pieces * BLOCK
    rows = GROUP * pieces
    whole = pl.BlockSpec(x.shape, lambda g, order: (0, 0, 0))
    return pl.pallas_call(
        lag_kernel,
        grid_spec=pltpu.PrefetchScalarGridSpec(
            num_scalar_prefetch=1,
            grid=(groups,),
            in_specs=[whole, whole],
            out_specs=pl.BlockSpec((groups, length), lambda g, order: (0, 0)),
            scratch_shapes=[
                pltpu.VMEM((rows, BLOCK), jnp.bfloat16),
                pltpu.VMEM((rows + BLOCK, BLOCK), jnp.bfloat16),
                pltpu.VMEM((BLOCK, length + BLOCK), jnp.float32),
                pltpu.VMEM((groups, length + BLOCK), jnp.float32),
            ],
        ),
        out_shape=jax.ShapeDtypeStruct((groups, length), jnp.float32),
        compiler_params=params(),
        cost_estimate=SHORT,
    )(order, x, w)


def post_kernel(
    r_hbm, a_hbm, b_hbm, x_hbm, y_hbm, r, a, b, x, y, r_sem, a_sem, b_sem, x_sem, y_sem
):
    into = list(
        zip(
            tile_copies(r_hbm, r, r_sem, CHUNKS),
            copies(a_hbm, a, a_sem, CHUNKS),
            copies(b_hbm, b, b_sem, CHUNKS),
            strict=True,
        )
    )
    back = list(
        zip(copies(x, x_hbm, x_sem, CHUNKS), copies(y, y_hbm, y_sem, CHUNKS), strict=True)
    )
    for group in into:
        for copy in group:
            copy.start()
    tiles = r.shape[0] // CHUNKS
    for i in range(CHUNKS):
        for copy in into[i]:
            copy.wait()
        for t in range(i * tiles, (i + 1) * tiles):
            cols = slice(t * BLOCK, (t + 1) * BLOCK)
            turned = r[t].T
            x[0, :, cols] = product_of(a[0, :, cols], turned)
            y[0, :, cols] = product_of(b[0, :, cols], turned)
        for copy in back[i]:
            copy.start()
    for group in back:
        for copy in group:
            copy.wait()


def post(r, a, b):
    anywhere = pl.BlockSpec(memory_space=pl.ANY)
    shape = jax.ShapeDtypeStruct(a.shape, a.dtype)
    return pl.pallas_call(
        post_kernel,
        in_specs=[anywhere] * 3,
        out_specs=[anywhere] * 2,
        out_shape=[shape, shape],
        scratch_shapes=[pltpu.VMEM(r.shape, r.dtype)]
        + [pltpu.VMEM(a.shape, a.dtype)] * 4
        + [pltpu.SemaphoreType.DMA((CHUNKS,))] * 5,
        compiler_params=params(24),
        cost_estimate=pl.CostEstimate(
            flops=2 * a.size, bytes_accessed=10 * a.size, transcendentals=0
        ),
    )(r, a, b)


def taps_kernel(sequences, taps_ref, mine_ref, others_ref, out_ref):
    taps = taps_ref[...]
    length = taps.shape[1]
    root = jnp.sqrt(jnp.mean(taps * taps, axis=1, keepdims=True) + EPSILON)
    scale = 1.0 / (math.sqrt(length) * root)
    mean = (mine_ref[...] + others_ref[...]) / sequences
    projection = jnp.sum(mean * taps, axis=1, keepdims=True)
    out_ref[...] = scale * mean - taps * (scale * scale * scale) * projection


def taps_grad_of(taps, mine, others, sequences):
    return pl.pallas_call(
        functools.partial(taps_kernel, sequences),
        out_shape=jax.ShapeDtypeStruct(taps.shape, jnp.float32),
        compiler_params=params(),
    )(taps, mine, others)


def exchange(tiles):
    return lax.all_to_all(tiles, "ctx", split_axis=0, concat_axis=0, tiled=True)


def from_partner(x, step):
    return lax.ppermute(x, "dp", [(i, i ^ step) for i in range(lax.axis_size("dp"))])


def shards(output_gate_input, key_input, value_input, upstream, filter_taps, order):
    groups = filter_taps.shape[0]
    sequences = lax.axis_size("dp")
    product_tiles = pre(key_input, value_input)
    product = exchange(product_tiles)
    weighted_tiles, strip = pre_and_strips(upstream, output_gate_input, filter_taps)
    weighted = exchange(weighted_tiles)
    mixing_tiles = conv(order, product, strip, False)
    mixing = exchange(mixing_tiles)
    product, _ = lax.optimization_barrier((product, mixing_tiles))
    lag_sums = lag_sums_of(order, product, weighted, groups)
    later, lag_sums = lax.optimization_barrier((weighted, lag_sums))
    near = [from_partner(lag_sums, step) for step in range(1, sequences // 2)]
    returned_tiles = conv(order, later, strip, True)
    half = sum(near, lag_sums)
    returned_tiles, half = lax.optimization_barrier((returned_tiles, half))
    returned = exchange(returned_tiles)
    far = from_partner(half, sequences // 2)
    mixed_out, gate_grad = post(mixing, output_gate_input, upstream)
    half, mixed_out = lax.optimization_barrier((half, mixed_out))
    taps_grad = taps_grad_of(filter_taps, half, far, sequences)
    key_grad, value_grad = post(returned, value_input, key_input)
    return mixed_out, gate_grad, key_grad, value_grad, taps_grad


def solution(mesh):
    rows = P("dp", "ctx", None)
    return jax.shard_map(
        shards,
        mesh=mesh,
        in_specs=(rows, rows, rows, rows, P("ctx", None), P()),
        out_specs=(rows, rows, rows, rows, P("ctx", None)),
        check_vma=False,
    )
```

```python
import functools
import math

import jax
import jax.numpy as jnp
from jax import lax
from jax.experimental import pallas as pl
from jax.experimental.pallas import tpu as pltpu
from jax.sharding import PartitionSpec as P

EPSILON = 1e-06
BLOCK = 128
GROUP = 16
MIB = 1024 * 1024
SPAN = 4
AT_ONCE = 4
CHUNKS = 4

SHORT = pl.CostEstimate(flops=1000, bytes_accessed=1000, transcendentals=0)
LONG = pl.CostEstimate(flops=10**10, bytes_accessed=1000, transcendentals=0)

NN = (((1,), (0,)), ((), ()))
NT = (((1,), (1,)), ((), ()))
TN = (((0,), (0,)), ((), ()))


def dot(a, b, dims):
    return lax.dot_general(a, b, dims, preferred_element_type=jnp.float32)


def params(mib=60):
    return pltpu.CompilerParams(vmem_limit_bytes=mib * MIB)


def product_of(a, b):
    return a * b


def copies(source, target, sems, chunks):
    step = source.shape[-1] // chunks
    made = []
    for i in range(chunks):
        cols = pl.ds(i * step, step)
        made.append(
            pltpu.make_async_copy(source.at[0, :, cols], target.at[0, :, cols], sems.at[i])
        )
    return made


def tile_copies(source, target, sems, chunks):
    step = source.shape[0] // chunks
    made = []
    for i in range(chunks):
        part = pl.ds(i * step, step)
        made.append(pltpu.make_async_copy(source.at[part], target.at[part], sems.at[i]))
    return made


def pre_kernel(a_hbm, b_hbm, out_hbm, a, b, out, a_sem, b_sem, out_sem):
    into = list(
        zip(copies(a_hbm, a, a_sem, CHUNKS), copies(b_hbm, b, b_sem, CHUNKS), strict=True)
    )
    back = tile_copies(out, out_hbm, out_sem, CHUNKS)
    for pair in into:
        for copy in pair:
            copy.start()
    tiles = out.shape[0] // CHUNKS
    for i in range(CHUNKS):
        for copy in into[i]:
            copy.wait()
        for t in range(i * tiles, (i + 1) * tiles):
            cols = slice(t * BLOCK, (t + 1) * BLOCK)
            out[t] = product_of(a[0, :, cols], b[0, :, cols]).T
        back[i].start()
    for copy in back:
        copy.wait()


def pre(a, b):
    _, rows, channels = a.shape
    tiles = (channels // BLOCK, BLOCK, rows)
    anywhere = pl.BlockSpec(memory_space=pl.ANY)
    return pl.pallas_call(
        pre_kernel,
        in_specs=[anywhere, anywhere],
        out_specs=anywhere,
        out_shape=jax.ShapeDtypeStruct(tiles, jnp.bfloat16),
        scratch_shapes=[
            pltpu.VMEM(a.shape, jnp.bfloat16),
            pltpu.VMEM(b.shape, jnp.bfloat16),
            pltpu.VMEM(tiles, jnp.bfloat16),
        ]
        + [pltpu.SemaphoreType.DMA((CHUNKS,))] * 3,
        compiler_params=params(),
        cost_estimate=pl.CostEstimate(
            flops=a.size, bytes_accessed=6 * a.size, transcendentals=0
        ),
    )(a, b)


def strip_kernel(taps_ref, out_ref):
    g = pl.program_id(0)
    taps = taps_ref[pl.ds(g, 1), :]
    length = taps.shape[1]
    root = jnp.sqrt(jnp.mean(taps * taps, axis=1, keepdims=True) + EPSILON)
    row = taps * (1.0 / (math.sqrt(length) * root))
    width = length + BLOCK
    cur = jnp.concatenate([jnp.zeros((1, BLOCK), jnp.float32), row], axis=1)
    cur = jnp.broadcast_to(cur, (16, width))
    line = lax.broadcasted_iota(jnp.int32, (16, width), 0)
    for step in (1, 2, 4, 8):
        cur = jnp.where((line & step) != 0, pltpu.roll(cur, step, 1), cur)
    for q in range(BLOCK // 16):
        if q:
            cur = pltpu.roll(cur, 16, 1)
        out_ref[0, 16 * q : 16 * (q + 1), :] = cur.astype(jnp.bfloat16)
    out_ref[0, :, :BLOCK] = jnp.zeros((BLOCK, BLOCK), jnp.bfloat16)


def pre_strip_kernel(tiles, a_ref, b_ref, taps_ref, out_ref, strip_ref):
    for i in range(tiles):
        cols = slice(i * BLOCK, (i + 1) * BLOCK)
        out_ref[i] = product_of(a_ref[0, :, cols], b_ref[0, :, cols]).T
    strip_kernel(taps_ref, strip_ref)


def pre_and_strips(a, b, taps):
    _, rows, channels = a.shape
    pieces = channels // BLOCK
    groups, length = taps.shape
    tiles = pieces // groups
    width = length + BLOCK
    spec = pl.BlockSpec((1, rows, tiles * BLOCK), lambda i: (0, 0, i))
    return pl.pallas_call(
        functools.partial(pre_strip_kernel, tiles),
        grid=(groups,),
        in_specs=[spec, spec, pl.BlockSpec((groups, length), lambda i: (0, 0))],
        out_specs=[
            pl.BlockSpec((tiles, BLOCK, rows), lambda i: (i, 0, 0)),
            pl.BlockSpec((1, BLOCK, width), lambda i: (i, 0, 0)),
        ],
        out_shape=[
            jax.ShapeDtypeStruct((pieces, BLOCK, rows), jnp.bfloat16),
            jax.ShapeDtypeStruct((groups, BLOCK, width), jnp.bfloat16),
        ],
        compiler_params=params(),
        cost_estimate=pl.CostEstimate(
            flops=4 * groups * BLOCK * width,
            bytes_accessed=2 * groups * BLOCK * width + 6 * a.size,
            transcendentals=0,
        ),
    )(a, b, taps)


def in_order(order_ref, source, target, sems):
    return [
        pltpu.make_async_copy(source.at[d], target.at[order_ref[d]], sems.at[d])
        for d in range(source.shape[0])
    ]


def start(made):
    for copy in made:
        copy.start()


def wait(made):
    for copy in made:
        copy.wait()


def rows_of(group):
    first = GROUP * group
    return pl.ds(first if isinstance(first, int) else pl.multiple_of(first, GROUP), GROUP)


def forward_kernel(
    order_ref, x_hbm, strip_hbm, out_hbm, x, strip, out, acc, x_sem, s_sem, out_sem
):
    groups = strip.shape[0]
    arrive = in_order(order_ref, x_hbm, x, x_sem)
    start(arrive)
    strips = [
        pltpu.make_async_copy(strip_hbm.at[g], strip.at[g], s_sem.at[g]) for g in range(groups)
    ]
    start(strips)
    wait(arrive)

    def ready(g):
        pltpu.make_async_copy(strip_hbm.at[g], strip.at[g], s_sem.at[g]).wait()

    filter_groups(False, x, strip, out, acc, ready)
    send(order_ref, out, out_hbm, out_sem)


def back_kernel(order_ref, x, strip, out_hbm, out, acc, out_sem):
    filter_groups(True, x, strip, out, acc, lambda g: None)
    send(order_ref, out, out_hbm, out_sem)


def send(order_ref, out, out_hbm, out_sem):
    leave = [
        pltpu.make_async_copy(out.at[order_ref[d]], out_hbm.at[d], out_sem.at[d])
        for d in range(out.shape[0])
    ]
    start(leave)
    wait(leave)


def filter_groups(backward, x, strip, out, acc, ready):
    pieces = x.shape[0]
    groups = strip.shape[0]
    pairs = pieces // 2
    wide = 2 * BLOCK
    nothing = jnp.zeros((GROUP, wide), jnp.bfloat16)
    @pl.loop(0, groups)
    def _(g):
        ready(g)
        blocks = [
            jnp.concatenate([x[2 * i, rows_of(g), :], x[2 * i + 1, rows_of(g), :]], axis=1)
            for i in range(pairs)
        ]
        for lag in range(0, pairs, SPAN):
            at = BLOCK + wide * lag
            lefts, weights = [], []
            for k in range(min(SPAN, pairs - lag)):
                if backward:
                    froms = range(lag + k, pairs + k)
                else:
                    froms = range(-k, pairs - lag - k)
                lefts.append(
                    jnp.concatenate(
                        [blocks[i] if 0 <= i < pairs else nothing for i in froms], axis=0
                    )
                )
                weights += [
                    strip[g, :, at + wide * k : at + wide * (k + 1)],
                    strip[g, :, at + wide * k - BLOCK : at + wide * k + BLOCK],
                ]
            if backward:
                ends = at + wide * min(SPAN, pairs - lag)
                weights = [strip[g, :, at:ends], strip[g, :, at - BLOCK : ends - BLOCK]]
            part = dot(
                jnp.concatenate(lefts, axis=1),
                jnp.concatenate(weights, axis=0),
                NT if backward else NN,
            )
            depth = GROUP * (pairs - lag)
            if lag == 0:
                acc[0] = part
            elif backward:
                acc[0, :depth, :] += part
            else:
                acc[0, GROUP * lag :, :] += part
        for i in range(pairs):
            both = acc[0, rows_of(i), :].astype(jnp.bfloat16)
            out[2 * i, rows_of(g), :] = both[:, :BLOCK]
            out[2 * i + 1, rows_of(g), :] = both[:, BLOCK:]


def forward(order, x, strip):
    pieces = x.shape[0]
    groups = strip.shape[0]
    rows = GROUP * pieces // 2
    anywhere = pl.BlockSpec(memory_space=pl.ANY)
    return pl.pallas_call(
        forward_kernel,
        in_specs=[pl.BlockSpec(memory_space=pltpu.SMEM), anywhere, anywhere],
        out_specs=anywhere,
        scratch_shapes=[
            pltpu.VMEM(x.shape, x.dtype),
            pltpu.VMEM(strip.shape, strip.dtype),
            pltpu.VMEM(x.shape, x.dtype),
            pltpu.VMEM((2, rows, 2 * BLOCK), jnp.float32),
            pltpu.SemaphoreType.DMA((pieces,)),
            pltpu.SemaphoreType.DMA((groups,)),
            pltpu.SemaphoreType.DMA((pieces,)),
        ],
        out_shape=jax.ShapeDtypeStruct(x.shape, jnp.bfloat16),
        compiler_params=params(),
        cost_estimate=SHORT,
    )(order, x, strip)


def back(order, x, strip):
    pieces = x.shape[0]
    vmem = pl.BlockSpec(memory_space=pltpu.VMEM)
    return pl.pallas_call(
        back_kernel,
        in_specs=[pl.BlockSpec(memory_space=pltpu.SMEM), vmem, vmem],
        out_specs=pl.BlockSpec(memory_space=pl.ANY),
        scratch_shapes=[
            pltpu.VMEM(x.shape, x.dtype),
            pltpu.VMEM((2, GROUP * pieces // 2, 2 * BLOCK), jnp.float32),
            pltpu.SemaphoreType.DMA((pieces,)),
        ],
        out_shape=pltpu.HBM(x.shape, jnp.bfloat16),
        compiler_params=params(50),
        cost_estimate=LONG,
    )(
        order,
        pltpu.with_memory_space_constraint(x, pltpu.VMEM),
        pltpu.with_memory_space_constraint(strip, pltpu.VMEM),
    )


def lag_kernel(
    order_ref, x_hbm, w_hbm, strip_hbm, out_ref, w, strip, x, squares, sums, x_sem, w_sem, s_sem
):
    pieces = x.shape[0]
    groups = out_ref.shape[0]
    total = GROUP * pieces
    last = BLOCK - 1
    arrive = in_order(order_ref, x_hbm, x, x_sem) + in_order(order_ref, w_hbm, w, w_sem)
    start(arrive)
    kept = pltpu.make_async_copy(strip_hbm, strip, s_sem)
    kept.start()
    row = lax.broadcasted_iota(jnp.int32, (BLOCK, BLOCK), 0)
    col = lax.broadcasted_iota(jnp.int32, (BLOCK, BLOCK), 1)
    mirror = jnp.where(row + col == last, 1.0, 0.0).astype(jnp.bfloat16)
    nothing = jnp.zeros((GROUP, BLOCK), jnp.bfloat16)
    for i in range(2):
        squares[i, :, pieces * BLOCK :] = jnp.zeros((BLOCK, BLOCK), jnp.float32)
    wait(arrive)
    def one(g, here):
        xs = jnp.concatenate([x[j, rows_of(g), :] for j in range(pieces)], axis=0)
        x_turned = dot(mirror, xs, NT).astype(jnp.bfloat16)
        blocks = [w[j, rows_of(g), :] for j in range(pieces)]
        for lag in range(0, pieces, 2):
            depth = total - GROUP * lag // BLOCK * BLOCK
            right = jnp.concatenate(
                [
                    jnp.concatenate(
                        [
                            blocks[j] if j < pieces else nothing
                            for j in range(first, first + depth // GROUP)
                        ],
                        axis=0,
                    )
                    for first in (lag, lag + 1)
                ],
                axis=1,
            )
            squares[here, :, lag * BLOCK : (lag + 2) * BLOCK] = dot(
                x_turned[:, :depth], right, NN
            )
        step = 8
        for t in range(0, pieces, step):
            cols = slice(t * BLOCK, (t + step + 1) * BLOCK)
            added = None
            for q in range(BLOCK // 8):
                moved = pltpu.roll(
                    squares[here, 8 * q : 8 * q + 8, cols], 8 * q, 1, stride=1, stride_axis=0
                )
                added = moved if added is None else added + moved
            added = jnp.sum(added, axis=0, keepdims=True)
            skip = BLOCK if t else 0
            sums[pl.ds(g, 1), t * BLOCK + skip : (t + step + 1) * BLOCK] = added[:, skip:]

    @pl.loop(0, groups // AT_ONCE)
    def _(i):
        for k in range(AT_ONCE):
            one(i * AT_ONCE + k, k % 2)

    width = sums.shape[1]
    out_ref[...] = pltpu.roll(sums[...], width - last, 1)[:, : pieces * BLOCK]
    kept.wait()


def lag_sums_of(order, x, w, strip):
    pieces = x.shape[0]
    groups = strip.shape[0]
    length = pieces * BLOCK
    anywhere = pl.BlockSpec(memory_space=pl.ANY)
    vmem = pl.BlockSpec(memory_space=pltpu.VMEM)
    return pl.pallas_call(
        lag_kernel,
        in_specs=[pl.BlockSpec(memory_space=pltpu.SMEM), anywhere, anywhere, anywhere],
        out_specs=[vmem, vmem, vmem],
        scratch_shapes=[
            pltpu.VMEM(x.shape, x.dtype),
            pltpu.VMEM((2, BLOCK, length + BLOCK), jnp.float32),
            pltpu.VMEM((groups, length + BLOCK), jnp.float32),
            pltpu.SemaphoreType.DMA((pieces,)),
            pltpu.SemaphoreType.DMA((pieces,)),
            pltpu.SemaphoreType.DMA,
        ],
        out_shape=[
            jax.ShapeDtypeStruct((groups, length), jnp.float32),
            pltpu.VMEM(w.shape, w.dtype),
            pltpu.VMEM(strip.shape, strip.dtype),
        ],
        compiler_params=params(50),
        cost_estimate=SHORT,
    )(
        order,
        pltpu.with_memory_space_constraint(x, pltpu.HBM),
        w,
        pltpu.with_memory_space_constraint(strip, pltpu.HBM),
    )


def post_kernel(
    r_hbm, a_hbm, b_hbm, x_hbm, y_hbm, r, a, b, x, y, r_sem, a_sem, b_sem, x_sem, y_sem
):
    into = list(
        zip(
            tile_copies(r_hbm, r, r_sem, CHUNKS),
            copies(a_hbm, a, a_sem, CHUNKS),
            copies(b_hbm, b, b_sem, CHUNKS),
            strict=True,
        )
    )
    back = list(
        zip(copies(x, x_hbm, x_sem, CHUNKS), copies(y, y_hbm, y_sem, CHUNKS), strict=True)
    )
    for group in into:
        for copy in group:
            copy.start()
    tiles = r.shape[0] // CHUNKS
    for i in range(CHUNKS):
        for copy in into[i]:
            copy.wait()
        for t in range(i * tiles, (i + 1) * tiles):
            cols = slice(t * BLOCK, (t + 1) * BLOCK)
            turned = r[t].T
            x[0, :, cols] = product_of(a[0, :, cols], turned)
            y[0, :, cols] = product_of(b[0, :, cols], turned)
        for copy in back[i]:
            copy.start()
    for group in back:
        for copy in group:
            copy.wait()


def post(r, a, b):
    anywhere = pl.BlockSpec(memory_space=pl.ANY)
    shape = jax.ShapeDtypeStruct(a.shape, a.dtype)
    return pl.pallas_call(
        post_kernel,
        in_specs=[anywhere] * 3,
        out_specs=[anywhere] * 2,
        out_shape=[shape, shape],
        scratch_shapes=[pltpu.VMEM(r.shape, r.dtype)]
        + [pltpu.VMEM(a.shape, a.dtype)] * 4
        + [pltpu.SemaphoreType.DMA((CHUNKS,))] * 5,
        compiler_params=params(24),
        cost_estimate=pl.CostEstimate(
            flops=2 * a.size, bytes_accessed=10 * a.size, transcendentals=0
        ),
    )(r, a, b)


def taps_kernel(sequences, taps_ref, mine_ref, others_ref, out_ref):
    taps = taps_ref[...]
    length = taps.shape[1]
    root = jnp.sqrt(jnp.mean(taps * taps, axis=1, keepdims=True) + EPSILON)
    scale = 1.0 / (math.sqrt(length) * root)
    mean = (mine_ref[...] + others_ref[...]) / sequences
    projection = jnp.sum(mean * taps, axis=1, keepdims=True)
    out_ref[...] = scale * mean - taps * (scale * scale * scale) * projection


def taps_grad_of(taps, mine, others, sequences):
    return pl.pallas_call(
        functools.partial(taps_kernel, sequences),
        out_shape=jax.ShapeDtypeStruct(taps.shape, jnp.float32),
        compiler_params=params(),
    )(taps, mine, others)


def exchange(tiles):
    return lax.all_to_all(tiles, "ctx", split_axis=0, concat_axis=0, tiled=True)


def from_partner(x, step):
    return lax.ppermute(x, "dp", [(i, i ^ step) for i in range(lax.axis_size("dp"))])


def shards(output_gate_input, key_input, value_input, upstream, filter_taps, order):
    sequences = lax.axis_size("dp")
    product_tiles = pre(key_input, value_input)
    product = exchange(product_tiles)
    weighted_tiles, strip = pre_and_strips(upstream, output_gate_input, filter_taps)
    weighted = exchange(weighted_tiles)
    mixing_tiles = forward(order, product, strip)
    mixing = exchange(mixing_tiles)
    product, _ = lax.optimization_barrier((product, mixing_tiles))
    lag_sums, weighted_kept, strip_kept = lag_sums_of(order, product, weighted, strip)
    near = [from_partner(lag_sums, step) for step in range(1, sequences // 2)]
    returned_tiles = back(order, weighted_kept, strip_kept)
    half = sum(near, lag_sums)
    returned_tiles, half = lax.optimization_barrier((returned_tiles, half))
    returned = exchange(returned_tiles)
    far = from_partner(half, sequences // 2)
    mixed_out, gate_grad = post(mixing, output_gate_input, upstream)
    half, mixed_out = lax.optimization_barrier((half, mixed_out))
    taps_grad = taps_grad_of(filter_taps, half, far, sequences)
    key_grad, value_grad = post(returned, value_input, key_input)
    return mixed_out, gate_grad, key_grad, value_grad, taps_grad


def solution(mesh):
    rows = P("dp", "ctx", None)
    return jax.shard_map(
        shards,
        mesh=mesh,
        in_specs=(rows, rows, rows, rows, P("ctx", None), P()),
        out_specs=(rows, rows, rows, rows, P("ctx", None)),
        check_vma=False,
    )
```

```python
import functools
import math

import jax
import jax.numpy as jnp
from jax import lax
from jax.experimental import pallas as pl
from jax.experimental.pallas import tpu as pltpu
from jax.sharding import PartitionSpec as P

EPSILON = 1e-06
BLOCK = 128
GROUP = 16
MIB = 1024 * 1024
SPAN = 1
AT_ONCE = 8
CHUNKS = 4

SHORT = pl.CostEstimate(flops=1000, bytes_accessed=1000, transcendentals=0)
LONG = pl.CostEstimate(flops=10**10, bytes_accessed=1000, transcendentals=0)

NN = (((1,), (0,)), ((), ()))
NT = (((1,), (1,)), ((), ()))
TN = (((0,), (0,)), ((), ()))


def dot(a, b, dims):
    return lax.dot_general(a, b, dims, preferred_element_type=jnp.float32)


def params(mib=60):
    return pltpu.CompilerParams(vmem_limit_bytes=mib * MIB)


def product_of(a, b):
    return a * b


def copies(source, target, sems, chunks):
    step = source.shape[-1] // chunks
    made = []
    for i in range(chunks):
        cols = pl.ds(i * step, step)
        made.append(
            pltpu.make_async_copy(source.at[0, :, cols], target.at[0, :, cols], sems.at[i])
        )
    return made


def tile_copies(source, target, sems, chunks):
    step = source.shape[0] // chunks
    made = []
    for i in range(chunks):
        part = pl.ds(i * step, step)
        made.append(pltpu.make_async_copy(source.at[part], target.at[part], sems.at[i]))
    return made


def pre_kernel(a_hbm, b_hbm, c_hbm, d_hbm, out_hbm, a, b, c, d, out, in_sem, out_sem):
    into = list(
        zip(
            *[
                copies(source, target, in_sem.at[k], CHUNKS)
                for k, (source, target) in enumerate(
                    ((a_hbm, a), (b_hbm, b), (c_hbm, c), (d_hbm, d))
                )
            ],
            strict=True,
        )
    )
    leave = tile_copies(out, out_hbm, out_sem, CHUNKS)
    for group in into:
        start(group)
    tiles = out.shape[0] // CHUNKS
    for i in range(CHUNKS):
        wait(into[i])
        for t in range(i * tiles, (i + 1) * tiles):
            cols = slice(t * BLOCK, (t + 1) * BLOCK)
            out[t, :BLOCK, :] = product_of(a[0, :, cols], b[0, :, cols]).T
            out[t, BLOCK:, :] = product_of(c[0, :, cols], d[0, :, cols]).T
        leave[i].start()
    wait(leave)


def pre(a, b, c, d):
    _, rows, channels = a.shape
    tiles = (channels // BLOCK, 2 * BLOCK, rows)
    anywhere = pl.BlockSpec(memory_space=pl.ANY)
    return pl.pallas_call(
        pre_kernel,
        in_specs=[anywhere] * 4,
        out_specs=anywhere,
        out_shape=jax.ShapeDtypeStruct(tiles, jnp.bfloat16),
        scratch_shapes=[pltpu.VMEM(a.shape, jnp.bfloat16)] * 4
        + [
            pltpu.VMEM(tiles, jnp.bfloat16),
            pltpu.SemaphoreType.DMA((4, CHUNKS)),
            pltpu.SemaphoreType.DMA((CHUNKS,)),
        ],
        compiler_params=params(),
        cost_estimate=pl.CostEstimate(
            flops=2 * a.size, bytes_accessed=12 * a.size, transcendentals=0
        ),
    )(a, b, c, d)


def strip_kernel(taps_ref, out_ref):
    g = pl.program_id(0)
    taps = taps_ref[pl.ds(g, 1), :]
    length = taps.shape[1]
    root = jnp.sqrt(jnp.mean(taps * taps, axis=1, keepdims=True) + EPSILON)
    row = taps * (1.0 / (math.sqrt(length) * root))
    width = length + BLOCK
    cur = jnp.concatenate([jnp.zeros((1, BLOCK), jnp.float32), row], axis=1)
    cur = jnp.broadcast_to(cur, (16, width))
    line = lax.broadcasted_iota(jnp.int32, (16, width), 0)
    for step in (1, 2, 4, 8):
        cur = jnp.where((line & step) != 0, pltpu.roll(cur, step, 1), cur)
    for q in range(BLOCK // 16):
        if q:
            cur = pltpu.roll(cur, 16, 1)
        out_ref[0, 16 * q : 16 * (q + 1), :] = cur.astype(jnp.bfloat16)
    out_ref[0, :, :BLOCK] = jnp.zeros((BLOCK, BLOCK), jnp.bfloat16)


def strips(taps):
    groups, length = taps.shape
    width = length + BLOCK
    return pl.pallas_call(
        strip_kernel,
        grid=(groups,),
        in_specs=[pl.BlockSpec((groups, length), lambda g: (0, 0))],
        out_specs=pl.BlockSpec((1, BLOCK, width), lambda g: (g, 0, 0)),
        out_shape=jax.ShapeDtypeStruct((groups, BLOCK, width), jnp.bfloat16),
        compiler_params=params(),
        cost_estimate=LONG,
    )(taps)


def in_order(order_ref, source, target, sems):
    return [
        pltpu.make_async_copy(source.at[d], target.at[order_ref[d]], sems.at[d])
        for d in range(source.shape[0])
    ]


def start(made):
    for copy in made:
        copy.start()


def wait(made):
    for copy in made:
        copy.wait()


def rows_of(group):
    first = GROUP * group
    return pl.ds(first if isinstance(first, int) else pl.multiple_of(first, GROUP), GROUP)


def filters_kernel(order_ref, x_hbm, strip_hbm, out_hbm, x, strip, out, acc, x_sem, s_sem, out_sem):
    groups = strip.shape[0]
    arrive = in_order(order_ref, x_hbm, x, x_sem)
    start(arrive)
    for g in range(groups):
        pltpu.make_async_copy(strip_hbm.at[g], strip.at[g], s_sem.at[g]).start()
    wait(arrive)

    @pl.loop(0, groups)
    def _(g):
        pltpu.make_async_copy(strip_hbm.at[g], strip.at[g], s_sem.at[g]).wait()
        filter_group(False, g, 0, x, strip, out, acc.at[0])
        filter_group(True, g, groups, x, strip, out, acc.at[1])

    leave = [
        pltpu.make_async_copy(out.at[order_ref[d]], out_hbm.at[d], out_sem.at[d])
        for d in range(out.shape[0])
    ]
    start(leave)
    wait(leave)


def filter_group(backward, g, shift, x, strip, out, acc):
    pieces = x.shape[0]
    pairs = pieces // 2
    wide = 2 * BLOCK
    nothing = jnp.zeros((GROUP, wide), jnp.bfloat16)
    rows = rows_of(g + shift)
    blocks = [
        jnp.concatenate([x[2 * i, rows, :], x[2 * i + 1, rows, :]], axis=1)
        for i in range(pairs)
    ]
    for lag in range(0, pairs, SPAN):
        at = BLOCK + wide * lag
        lefts, weights = [], []
        for k in range(min(SPAN, pairs - lag)):
            if backward:
                froms = range(lag + k, pairs + k)
            else:
                froms = range(-k, pairs - lag - k)
            lefts.append(
                jnp.concatenate(
                    [blocks[i] if 0 <= i < pairs else nothing for i in froms], axis=0
                )
            )
            weights += [
                strip[g, :, at + wide * k : at + wide * (k + 1)],
                strip[g, :, at + wide * k - BLOCK : at + wide * k + BLOCK],
            ]
        if backward:
            ends = at + wide * min(SPAN, pairs - lag)
            weights = [strip[g, :, at:ends], strip[g, :, at - BLOCK : ends - BLOCK]]
        part = dot(
            jnp.concatenate(lefts, axis=1),
            jnp.concatenate(weights, axis=0),
            NT if backward else NN,
        )
        depth = GROUP * (pairs - lag)
        if lag == 0:
            acc[...] = part
        elif backward:
            acc[:depth, :] += part
        else:
            acc[GROUP * lag :, :] += part
    for i in range(pairs):
        both = acc[rows_of(i), :].astype(jnp.bfloat16)
        out[2 * i, rows, :] = both[:, :BLOCK]
        out[2 * i + 1, rows, :] = both[:, BLOCK:]


def filters(order, x, strip):
    pieces = x.shape[0]
    groups = strip.shape[0]
    rows = GROUP * pieces // 2
    anywhere = pl.BlockSpec(memory_space=pl.ANY)
    return pl.pallas_call(
        filters_kernel,
        in_specs=[pl.BlockSpec(memory_space=pltpu.SMEM), anywhere, anywhere],
        out_specs=anywhere,
        scratch_shapes=[
            pltpu.VMEM(x.shape, x.dtype),
            pltpu.VMEM(strip.shape, strip.dtype),
            pltpu.VMEM(x.shape, x.dtype),
            pltpu.VMEM((2, rows, 2 * BLOCK), jnp.float32),
            pltpu.SemaphoreType.DMA((pieces,)),
            pltpu.SemaphoreType.DMA((groups,)),
            pltpu.SemaphoreType.DMA((pieces,)),
        ],
        out_shape=pltpu.HBM(x.shape, x.dtype),
        compiler_params=params(40),
        cost_estimate=LONG,
    )(order, x, pltpu.with_memory_space_constraint(strip, pltpu.HBM))


def lag_kernel(order_ref, x_hbm, out_ref, x, squares, sums, x_sem):
    pieces = x.shape[0]
    groups = out_ref.shape[0]
    total = GROUP * pieces
    last = BLOCK - 1
    arrive = in_order(order_ref, x_hbm, x, x_sem)
    start(arrive)
    row = lax.broadcasted_iota(jnp.int32, (BLOCK, BLOCK), 0)
    col = lax.broadcasted_iota(jnp.int32, (BLOCK, BLOCK), 1)
    mirror = jnp.where(row + col == last, 1.0, 0.0).astype(jnp.bfloat16)
    nothing = jnp.zeros((GROUP, BLOCK), jnp.bfloat16)
    for i in range(2):
        squares[i, :, pieces * BLOCK :] = jnp.zeros((BLOCK, BLOCK), jnp.float32)
    wait(arrive)
    def one(g, here):
        xs = jnp.concatenate([x[j, rows_of(g), :] for j in range(pieces)], axis=0)
        x_turned = dot(mirror, xs, NT).astype(jnp.bfloat16)
        blocks = [x[j, rows_of(g + groups), :] for j in range(pieces)]
        for lag in range(0, pieces, 2):
            depth = total - GROUP * lag // BLOCK * BLOCK
            right = jnp.concatenate(
                [
                    jnp.concatenate(
                        [
                            blocks[j] if j < pieces else nothing
                            for j in range(first, first + depth // GROUP)
                        ],
                        axis=0,
                    )
                    for first in (lag, lag + 1)
                ],
                axis=1,
            )
            squares[here, :, lag * BLOCK : (lag + 2) * BLOCK] = dot(
                x_turned[:, :depth], right, NN
            )
        step = 8
        for t in range(0, pieces, step):
            cols = slice(t * BLOCK, (t + step + 1) * BLOCK)
            added = None
            for q in range(BLOCK // 8):
                moved = pltpu.roll(
                    squares[here, 8 * q : 8 * q + 8, cols], 8 * q, 1, stride=1, stride_axis=0
                )
                added = moved if added is None else added + moved
            added = jnp.sum(added, axis=0, keepdims=True)
            skip = BLOCK if t else 0
            sums[pl.ds(g, 1), t * BLOCK + skip : (t + step + 1) * BLOCK] = added[:, skip:]

    @pl.loop(0, groups // AT_ONCE)
    def _(i):
        for k in range(AT_ONCE):
            one(i * AT_ONCE + k, k % 2)

    width = sums.shape[1]
    out_ref[...] = pltpu.roll(sums[...], width - last, 1)[:, : pieces * BLOCK]


def lag_sums_of(order, x, groups):
    pieces = x.shape[0]
    length = pieces * BLOCK
    return pl.pallas_call(
        lag_kernel,
        in_specs=[
            pl.BlockSpec(memory_space=pltpu.SMEM),
            pl.BlockSpec(memory_space=pl.ANY),
        ],
        out_specs=pl.BlockSpec(memory_space=pltpu.VMEM),
        scratch_shapes=[
            pltpu.VMEM(x.shape, x.dtype),
            pltpu.VMEM((2, BLOCK, length + BLOCK), jnp.float32),
            pltpu.VMEM((groups, length + BLOCK), jnp.float32),
            pltpu.SemaphoreType.DMA((pieces,)),
        ],
        out_shape=jax.ShapeDtypeStruct((groups, length), jnp.float32),
        compiler_params=params(),
        cost_estimate=SHORT,
    )(order, pltpu.with_memory_space_constraint(x, pltpu.HBM))


def post_kernel(r_hbm, *refs):
    ins, outs = refs[:4], refs[4:8]
    r, here, made, r_sem, in_sem, out_sem = refs[8], refs[9:13], refs[13:17], *refs[17:]
    into = list(
        zip(
            tile_copies(r_hbm, r, r_sem, CHUNKS),
            *[copies(ins[k], here[k], in_sem.at[k], CHUNKS) for k in range(4)],
            strict=True,
        )
    )
    leave = list(
        zip(*[copies(made[k], outs[k], out_sem.at[k], CHUNKS) for k in range(4)], strict=True)
    )
    for group in into:
        start(group)
    tiles = r.shape[0] // CHUNKS
    for i in range(CHUNKS):
        wait(into[i])
        for t in range(i * tiles, (i + 1) * tiles):
            cols = slice(t * BLOCK, (t + 1) * BLOCK)
            for half in range(2):
                turned = r[t, half * BLOCK : (half + 1) * BLOCK, :].T
                for k in (2 * half, 2 * half + 1):
                    made[k][0, :, cols] = product_of(here[k][0, :, cols], turned)
        start(leave[i])
    for group in leave:
        wait(group)


def post(r, *factors):
    anywhere = pl.BlockSpec(memory_space=pl.ANY)
    a = factors[0]
    return pl.pallas_call(
        post_kernel,
        in_specs=[anywhere] * 5,
        out_specs=[anywhere] * 4,
        out_shape=[jax.ShapeDtypeStruct(a.shape, a.dtype)] * 4,
        scratch_shapes=[pltpu.VMEM(r.shape, r.dtype)]
        + [pltpu.VMEM(a.shape, a.dtype)] * 8
        + [
            pltpu.SemaphoreType.DMA((CHUNKS,)),
            pltpu.SemaphoreType.DMA((4, CHUNKS)),
            pltpu.SemaphoreType.DMA((4, CHUNKS)),
        ],
        compiler_params=params(40),
        cost_estimate=pl.CostEstimate(
            flops=4 * a.size, bytes_accessed=20 * a.size, transcendentals=0
        ),
    )(r, *[pltpu.with_memory_space_constraint(a, pltpu.HBM) for a in factors])


def taps_kernel(sequences, taps_ref, mine_ref, others_ref, out_ref):
    taps = taps_ref[...]
    length = taps.shape[1]
    root = jnp.sqrt(jnp.mean(taps * taps, axis=1, keepdims=True) + EPSILON)
    scale = 1.0 / (math.sqrt(length) * root)
    mean = (mine_ref[...] + others_ref[...]) / sequences
    projection = jnp.sum(mean * taps, axis=1, keepdims=True)
    out_ref[...] = scale * mean - taps * (scale * scale * scale) * projection


def taps_grad_of(taps, mine, others, sequences):
    return pl.pallas_call(
        functools.partial(taps_kernel, sequences),
        out_shape=jax.ShapeDtypeStruct(taps.shape, jnp.float32),
        compiler_params=params(),
    )(taps, mine, others)


def exchange(tiles):
    return lax.all_to_all(tiles, "ctx", split_axis=0, concat_axis=0, tiled=True)


def from_partner(x, step):
    return lax.ppermute(x, "dp", [(i, i ^ step) for i in range(lax.axis_size("dp"))])


def shards(output_gate_input, key_input, value_input, upstream, filter_taps, order):
    sequences = lax.axis_size("dp")
    arrived = exchange(pre(key_input, value_input, upstream, output_gate_input))
    strip = strips(filter_taps)
    filtered = filters(order, arrived, strip)
    returned = exchange(filtered)
    arrived, _ = lax.optimization_barrier((arrived, filtered))
    lag_sums = lag_sums_of(order, arrived, filter_taps.shape[0])
    near = [from_partner(lag_sums, step) for step in range(1, sequences // 2)]
    half = sum(near, lag_sums)
    far = from_partner(half, sequences // 2)
    mixed_out, gate_grad, key_grad, value_grad = post(
        returned, output_gate_input, upstream, value_input, key_input
    )
    half, mixed_out = lax.optimization_barrier((half, mixed_out))
    taps_grad = taps_grad_of(filter_taps, half, far, sequences)
    return mixed_out, gate_grad, key_grad, value_grad, taps_grad


def solution(mesh):
    rows = P("dp", "ctx", None)
    return jax.shard_map(
        shards,
        mesh=mesh,
        in_specs=(rows, rows, rows, rows, P("ctx", None), P()),
        out_specs=(rows, rows, rows, rows, P("ctx", None)),
        check_vma=False,
    )
```

```python
import functools
import math

import jax
import jax.numpy as jnp
from jax import lax
from jax.experimental import pallas as pl
from jax.experimental.pallas import tpu as pltpu
from jax.sharding import PartitionSpec as P

EPSILON = 1e-06
BLOCK = 128
GROUP = 16
MIB = 1024 * 1024
SPAN = 1
AT_ONCE = 8
CHUNKS = 4

SHORT = pl.CostEstimate(flops=1000, bytes_accessed=1000, transcendentals=0)
LONG = pl.CostEstimate(flops=10**10, bytes_accessed=1000, transcendentals=0)

NN = (((1,), (0,)), ((), ()))
NT = (((1,), (1,)), ((), ()))
TN = (((0,), (0,)), ((), ()))


def dot(a, b, dims):
    return lax.dot_general(a, b, dims, preferred_element_type=jnp.float32)


def params(mib=60):
    return pltpu.CompilerParams(vmem_limit_bytes=mib * MIB)


def product_of(a, b):
    return a * b


def copies(source, target, sems, chunks):
    step = source.shape[-1] // chunks
    made = []
    for i in range(chunks):
        cols = pl.ds(i * step, step)
        made.append(
            pltpu.make_async_copy(source.at[0, :, cols], target.at[0, :, cols], sems.at[i])
        )
    return made


def tile_copies(source, target, sems, chunks):
    step = source.shape[0] // chunks
    made = []
    for i in range(chunks):
        part = pl.ds(i * step, step)
        made.append(pltpu.make_async_copy(source.at[part], target.at[part], sems.at[i]))
    return made


def pre_kernel(a_hbm, b_hbm, c_hbm, d_hbm, out_hbm, a, b, c, d, out, in_sem, out_sem):
    into = list(
        zip(
            *[
                copies(source, target, in_sem.at[k], CHUNKS)
                for k, (source, target) in enumerate(
                    ((a_hbm, a), (b_hbm, b), (c_hbm, c), (d_hbm, d))
                )
            ],
            strict=True,
        )
    )
    leave = tile_copies(out, out_hbm, out_sem, CHUNKS)
    for group in into:
        start(group)
    tiles = out.shape[0] // CHUNKS
    for i in range(CHUNKS):
        wait(into[i])
        for t in range(i * tiles, (i + 1) * tiles):
            cols = slice(t * BLOCK, (t + 1) * BLOCK)
            out[t, :BLOCK, :] = product_of(a[0, :, cols], b[0, :, cols]).T
            out[t, BLOCK:, :] = product_of(c[0, :, cols], d[0, :, cols]).T
        leave[i].start()
    wait(leave)


def pre(a, b, c, d):
    _, rows, channels = a.shape
    tiles = (channels // BLOCK, 2 * BLOCK, rows)
    anywhere = pl.BlockSpec(memory_space=pl.ANY)
    return pl.pallas_call(
        pre_kernel,
        in_specs=[anywhere] * 4,
        out_specs=anywhere,
        out_shape=jax.ShapeDtypeStruct(tiles, jnp.bfloat16),
        scratch_shapes=[pltpu.VMEM(a.shape, jnp.bfloat16)] * 4
        + [
            pltpu.VMEM(tiles, jnp.bfloat16),
            pltpu.SemaphoreType.DMA((4, CHUNKS)),
            pltpu.SemaphoreType.DMA((CHUNKS,)),
        ],
        compiler_params=params(),
        cost_estimate=pl.CostEstimate(
            flops=2 * a.size, bytes_accessed=12 * a.size, transcendentals=0
        ),
    )(a, b, c, d)


def strip_kernel(taps_ref, out_ref):
    g = pl.program_id(0)
    taps = taps_ref[pl.ds(g, 1), :]
    length = taps.shape[1]
    root = jnp.sqrt(jnp.mean(taps * taps, axis=1, keepdims=True) + EPSILON)
    row = taps * (1.0 / (math.sqrt(length) * root))
    width = length + BLOCK
    cur = jnp.concatenate([jnp.zeros((1, BLOCK), jnp.float32), row], axis=1)
    cur = jnp.broadcast_to(cur, (16, width))
    line = lax.broadcasted_iota(jnp.int32, (16, width), 0)
    for step in (1, 2, 4, 8):
        cur = jnp.where((line & step) != 0, pltpu.roll(cur, step, 1), cur)
    for q in range(BLOCK // 16):
        if q:
            cur = pltpu.roll(cur, 16, 1)
        out_ref[0, 16 * q : 16 * (q + 1), :] = cur.astype(jnp.bfloat16)
    out_ref[0, :, :BLOCK] = jnp.zeros((BLOCK, BLOCK), jnp.bfloat16)


def strips(taps):
    groups, length = taps.shape
    width = length + BLOCK
    return pl.pallas_call(
        strip_kernel,
        grid=(groups,),
        in_specs=[pl.BlockSpec((groups, length), lambda g: (0, 0))],
        out_specs=pl.BlockSpec((1, BLOCK, width), lambda g: (g, 0, 0)),
        out_shape=jax.ShapeDtypeStruct((groups, BLOCK, width), jnp.bfloat16),
        compiler_params=params(),
        cost_estimate=LONG,
    )(taps)


def in_order(order_ref, source, target, sems):
    return [
        pltpu.make_async_copy(source.at[d], target.at[order_ref[d]], sems.at[d])
        for d in range(source.shape[0])
    ]


def start(made):
    for copy in made:
        copy.start()


def wait(made):
    for copy in made:
        copy.wait()


def rows_of(group):
    first = GROUP * group
    return pl.ds(first if isinstance(first, int) else pl.multiple_of(first, GROUP), GROUP)


def filters_kernel(order_ref, x_hbm, strip_hbm, out_hbm, x, strip, out, acc, x_sem, s_sem, out_sem):
    groups = strip.shape[0]
    arrive = in_order(order_ref, x_hbm, x, x_sem)
    start(arrive)
    for g in range(groups):
        pltpu.make_async_copy(strip_hbm.at[g], strip.at[g], s_sem.at[g]).start()
    wait(arrive)

    @pl.loop(0, groups)
    def _(g):
        pltpu.make_async_copy(strip_hbm.at[g], strip.at[g], s_sem.at[g]).wait()
        filter_group(False, g, 0, x, strip, out, acc.at[0])
        filter_group(True, g, groups, x, strip, out, acc.at[1])

    leave = [
        pltpu.make_async_copy(out.at[order_ref[d]], out_hbm.at[d], out_sem.at[d])
        for d in range(out.shape[0])
    ]
    start(leave)
    wait(leave)


def filter_group(backward, g, shift, x, strip, out, acc):
    pieces = x.shape[0]
    pairs = pieces // 2
    wide = 2 * BLOCK
    nothing = jnp.zeros((GROUP, wide), jnp.bfloat16)
    rows = rows_of(g + shift)
    blocks = [
        jnp.concatenate([x[2 * i, rows, :], x[2 * i + 1, rows, :]], axis=1)
        for i in range(pairs)
    ]
    for lag in range(0, pairs, SPAN):
        at = BLOCK + wide * lag
        lefts, weights = [], []
        for k in range(min(SPAN, pairs - lag)):
            if backward:
                froms = range(lag + k, pairs + k)
            else:
                froms = range(-k, pairs - lag - k)
            lefts.append(
                jnp.concatenate(
                    [blocks[i] if 0 <= i < pairs else nothing for i in froms], axis=0
                )
            )
            weights += [
                strip[g, :, at + wide * k : at + wide * (k + 1)],
                strip[g, :, at + wide * k - BLOCK : at + wide * k + BLOCK],
            ]
        if backward:
            ends = at + wide * min(SPAN, pairs - lag)
            weights = [strip[g, :, at:ends], strip[g, :, at - BLOCK : ends - BLOCK]]
        part = dot(
            jnp.concatenate(lefts, axis=1),
            jnp.concatenate(weights, axis=0),
            NT if backward else NN,
        )
        depth = GROUP * (pairs - lag)
        if lag == 0:
            acc[...] = part
        elif backward:
            acc[:depth, :] += part
        else:
            acc[GROUP * lag :, :] += part
    for i in range(pairs):
        both = acc[rows_of(i), :].astype(jnp.bfloat16)
        out[2 * i, rows, :] = both[:, :BLOCK]
        out[2 * i + 1, rows, :] = both[:, BLOCK:]


def filters(order, x, strip):
    pieces = x.shape[0]
    groups = strip.shape[0]
    rows = GROUP * pieces // 2
    anywhere = pl.BlockSpec(memory_space=pl.ANY)
    return pl.pallas_call(
        filters_kernel,
        in_specs=[pl.BlockSpec(memory_space=pltpu.SMEM), anywhere, anywhere],
        out_specs=anywhere,
        scratch_shapes=[
            pltpu.VMEM(x.shape, x.dtype),
            pltpu.VMEM(strip.shape, strip.dtype),
            pltpu.VMEM(x.shape, x.dtype),
            pltpu.VMEM((2, rows, 2 * BLOCK), jnp.float32),
            pltpu.SemaphoreType.DMA((pieces,)),
            pltpu.SemaphoreType.DMA((groups,)),
            pltpu.SemaphoreType.DMA((pieces,)),
        ],
        out_shape=pltpu.HBM(x.shape, x.dtype),
        compiler_params=params(40),
        cost_estimate=LONG,
    )(order, x, pltpu.with_memory_space_constraint(strip, pltpu.HBM))


def lag_kernel(order_ref, x_hbm, out_ref, x, squares, sums, x_sem):
    pieces = x.shape[0]
    groups = out_ref.shape[0]
    total = GROUP * pieces
    last = BLOCK - 1
    arrive = in_order(order_ref, x_hbm, x, x_sem)
    start(arrive)
    row = lax.broadcasted_iota(jnp.int32, (BLOCK, BLOCK), 0)
    col = lax.broadcasted_iota(jnp.int32, (BLOCK, BLOCK), 1)
    mirror = jnp.where(row + col == last, 1.0, 0.0).astype(jnp.bfloat16)
    nothing = jnp.zeros((GROUP, BLOCK), jnp.bfloat16)
    for i in range(2):
        squares[i, :, pieces * BLOCK :] = jnp.zeros((BLOCK, BLOCK), jnp.float32)
    wait(arrive)
    def one(g, here):
        xs = jnp.concatenate([x[j, rows_of(g), :] for j in range(pieces)], axis=0)
        x_turned = dot(mirror, xs, NT).astype(jnp.bfloat16)
        blocks = [x[j, rows_of(g + groups), :] for j in range(pieces)]
        for lag in range(0, pieces, 2):
            depth = total - GROUP * lag // BLOCK * BLOCK
            right = jnp.concatenate(
                [
                    jnp.concatenate(
                        [
                            blocks[j] if j < pieces else nothing
                            for j in range(first, first + depth // GROUP)
                        ],
                        axis=0,
                    )
                    for first in (lag, lag + 1)
                ],
                axis=1,
            )
            squares[here, :, lag * BLOCK : (lag + 2) * BLOCK] = dot(
                x_turned[:, :depth], right, NN
            )
        step = 8
        for t in range(0, pieces, step):
            cols = slice(t * BLOCK, (t + step + 1) * BLOCK)
            added = None
            for q in range(BLOCK // 8):
                moved = pltpu.roll(
                    squares[here, 8 * q : 8 * q + 8, cols], 8 * q, 1, stride=1, stride_axis=0
                )
                added = moved if added is None else added + moved
            added = jnp.sum(added, axis=0, keepdims=True)
            skip = BLOCK if t else 0
            sums[pl.ds(g, 1), t * BLOCK + skip : (t + step + 1) * BLOCK] = added[:, skip:]

    @pl.loop(0, groups // AT_ONCE)
    def _(i):
        for k in range(AT_ONCE):
            one(i * AT_ONCE + k, k % 2)

    width = sums.shape[1]
    out_ref[...] = pltpu.roll(sums[...], width - last, 1)[:, : pieces * BLOCK].astype(jnp.bfloat16)


def lag_sums_of(order, x, groups):
    pieces = x.shape[0]
    length = pieces * BLOCK
    return pl.pallas_call(
        lag_kernel,
        in_specs=[
            pl.BlockSpec(memory_space=pltpu.SMEM),
            pl.BlockSpec(memory_space=pl.ANY),
        ],
        out_specs=pl.BlockSpec(memory_space=pltpu.VMEM),
        scratch_shapes=[
            pltpu.VMEM(x.shape, x.dtype),
            pltpu.VMEM((2, BLOCK, length + BLOCK), jnp.float32),
            pltpu.VMEM((groups, length + BLOCK), jnp.float32),
            pltpu.SemaphoreType.DMA((pieces,)),
        ],
        out_shape=jax.ShapeDtypeStruct((groups, length), jnp.bfloat16),
        compiler_params=params(),
        cost_estimate=SHORT,
    )(order, pltpu.with_memory_space_constraint(x, pltpu.HBM))


def post_kernel(r_hbm, *refs):
    ins, outs = refs[:4], refs[4:8]
    r, here, made, r_sem, in_sem, out_sem = refs[8], refs[9:13], refs[13:17], *refs[17:]
    into = list(
        zip(
            tile_copies(r_hbm, r, r_sem, CHUNKS),
            *[copies(ins[k], here[k], in_sem.at[k], CHUNKS) for k in range(4)],
            strict=True,
        )
    )
    leave = list(
        zip(*[copies(made[k], outs[k], out_sem.at[k], CHUNKS) for k in range(4)], strict=True)
    )
    for group in into:
        start(group)
    tiles = r.shape[0] // CHUNKS
    for i in range(CHUNKS):
        wait(into[i])
        for t in range(i * tiles, (i + 1) * tiles):
            cols = slice(t * BLOCK, (t + 1) * BLOCK)
            for half in range(2):
                turned = r[t, half * BLOCK : (half + 1) * BLOCK, :].T
                for k in (2 * half, 2 * half + 1):
                    made[k][0, :, cols] = product_of(here[k][0, :, cols], turned)
        start(leave[i])
    for group in leave:
        wait(group)


def post(r, *factors):
    anywhere = pl.BlockSpec(memory_space=pl.ANY)
    a = factors[0]
    return pl.pallas_call(
        post_kernel,
        in_specs=[anywhere] * 5,
        out_specs=[anywhere] * 4,
        out_shape=[jax.ShapeDtypeStruct(a.shape, a.dtype)] * 4,
        scratch_shapes=[pltpu.VMEM(r.shape, r.dtype)]
        + [pltpu.VMEM(a.shape, a.dtype)] * 8
        + [
            pltpu.SemaphoreType.DMA((CHUNKS,)),
            pltpu.SemaphoreType.DMA((4, CHUNKS)),
            pltpu.SemaphoreType.DMA((4, CHUNKS)),
        ],
        compiler_params=params(40),
        cost_estimate=pl.CostEstimate(
            flops=4 * a.size, bytes_accessed=20 * a.size, transcendentals=0
        ),
    )(r, *[pltpu.with_memory_space_constraint(a, pltpu.HBM) for a in factors])


def taps_kernel(sequences, taps_ref, mine_ref, others_ref, out_ref):
    taps = taps_ref[...]
    length = taps.shape[1]
    root = jnp.sqrt(jnp.mean(taps * taps, axis=1, keepdims=True) + EPSILON)
    scale = 1.0 / (math.sqrt(length) * root)
    mean = (mine_ref[...] + others_ref[...]) / sequences
    projection = jnp.sum(mean * taps, axis=1, keepdims=True)
    out_ref[...] = scale * mean - taps * (scale * scale * scale) * projection


def taps_grad_of(taps, mine, others, sequences):
    return pl.pallas_call(
        functools.partial(taps_kernel, sequences),
        out_shape=jax.ShapeDtypeStruct(taps.shape, jnp.float32),
        compiler_params=params(16),
    )(taps, mine, others)


def exchange(tiles):
    return lax.all_to_all(tiles, "ctx", split_axis=0, concat_axis=0, tiled=True)


def from_partner(x, step):
    return lax.ppermute(x, "dp", [(i, i ^ step) for i in range(lax.axis_size("dp"))])


def shards(output_gate_input, key_input, value_input, upstream, filter_taps, order):
    sequences = lax.axis_size("dp")
    arrived = exchange(pre(key_input, value_input, upstream, output_gate_input))
    strip = strips(filter_taps)
    filtered = filters(order, arrived, strip)
    returned = exchange(filtered)
    arrived, _ = lax.optimization_barrier((arrived, filtered))
    lag_sums = lag_sums_of(order, arrived, filter_taps.shape[0])
    near = [from_partner(lag_sums, step) for step in range(1, sequences // 2)]
    half = sum((part.astype(jnp.float32) for part in near), lag_sums.astype(jnp.float32))
    far = from_partner(half, sequences // 2)
    mixed_out, gate_grad, key_grad, value_grad = post(
        returned, output_gate_input, upstream, value_input, key_input
    )
    half, mixed_out = lax.optimization_barrier((half, mixed_out))
    taps_grad = taps_grad_of(filter_taps, half, far, sequences)
    return mixed_out, gate_grad, key_grad, value_grad, taps_grad


def solution(mesh):
    rows = P("dp", "ctx", None)
    return jax.shard_map(
        shards,
        mesh=mesh,
        in_specs=(rows, rows, rows, rows, P("ctx", None), P()),
        out_specs=(rows, rows, rows, rows, P("ctx", None)),
        check_vma=False,
    )
```

```python
import functools
import math

import jax
import jax.numpy as jnp
from jax import lax
from jax.experimental import pallas as pl
from jax.experimental.pallas import tpu as pltpu
from jax.sharding import PartitionSpec as P

EPSILON = 1e-06
BLOCK = 128
GROUP = 16
MIB = 1024 * 1024
SPAN = 1
AT_ONCE = 8
CHUNKS = 4

SHORT = pl.CostEstimate(flops=1000, bytes_accessed=1000, transcendentals=0)
LONG = pl.CostEstimate(flops=10**10, bytes_accessed=1000, transcendentals=0)

NN = (((1,), (0,)), ((), ()))
NT = (((1,), (1,)), ((), ()))
TN = (((0,), (0,)), ((), ()))


def dot(a, b, dims):
    return lax.dot_general(a, b, dims, preferred_element_type=jnp.float32)


def params(mib=60):
    return pltpu.CompilerParams(vmem_limit_bytes=mib * MIB)


def product_of(a, b):
    return a * b


def copies(source, target, sems, chunks):
    step = source.shape[-1] // chunks
    made = []
    for i in range(chunks):
        cols = pl.ds(i * step, step)
        made.append(
            pltpu.make_async_copy(source.at[0, :, cols], target.at[0, :, cols], sems.at[i])
        )
    return made


def tile_copies(source, target, sems, chunks):
    step = source.shape[0] // chunks
    made = []
    for i in range(chunks):
        part = pl.ds(i * step, step)
        made.append(pltpu.make_async_copy(source.at[part], target.at[part], sems.at[i]))
    return made


def pre_kernel(a_hbm, b_hbm, c_hbm, d_hbm, out_hbm, a, b, c, d, out, in_sem, out_sem):
    into = list(
        zip(
            *[
                copies(source, target, in_sem.at[k], CHUNKS)
                for k, (source, target) in enumerate(
                    ((a_hbm, a), (b_hbm, b), (c_hbm, c), (d_hbm, d))
                )
            ],
            strict=True,
        )
    )
    leave = tile_copies(out, out_hbm, out_sem, CHUNKS)
    for group in into:
        start(group)
    tiles = out.shape[0] // CHUNKS
    for i in range(CHUNKS):
        wait(into[i])
        for t in range(i * tiles, (i + 1) * tiles):
            cols = slice(t * BLOCK, (t + 1) * BLOCK)
            out[t, :BLOCK, :] = product_of(a[0, :, cols], b[0, :, cols]).T
            out[t, BLOCK:, :] = product_of(c[0, :, cols], d[0, :, cols]).T
        leave[i].start()
    wait(leave)


def pre(a, b, c, d):
    _, rows, channels = a.shape
    tiles = (channels // BLOCK, 2 * BLOCK, rows)
    anywhere = pl.BlockSpec(memory_space=pl.ANY)
    return pl.pallas_call(
        pre_kernel,
        in_specs=[anywhere] * 4,
        out_specs=anywhere,
        out_shape=jax.ShapeDtypeStruct(tiles, jnp.bfloat16),
        scratch_shapes=[pltpu.VMEM(a.shape, jnp.bfloat16)] * 4
        + [
            pltpu.VMEM(tiles, jnp.bfloat16),
            pltpu.SemaphoreType.DMA((4, CHUNKS)),
            pltpu.SemaphoreType.DMA((CHUNKS,)),
        ],
        compiler_params=params(),
        cost_estimate=pl.CostEstimate(
            flops=2 * a.size, bytes_accessed=12 * a.size, transcendentals=0
        ),
    )(a, b, c, d)


def strip_kernel(taps_ref, out_ref):
    g = pl.program_id(0)
    taps = taps_ref[pl.ds(g, 1), :]
    length = taps.shape[1]
    root = jnp.sqrt(jnp.mean(taps * taps, axis=1, keepdims=True) + EPSILON)
    row = taps * (1.0 / (math.sqrt(length) * root))
    width = length + BLOCK
    cur = jnp.concatenate([jnp.zeros((1, BLOCK), jnp.float32), row], axis=1)
    cur = jnp.broadcast_to(cur, (16, width))
    line = lax.broadcasted_iota(jnp.int32, (16, width), 0)
    for step in (1, 2, 4, 8):
        cur = jnp.where((line & step) != 0, pltpu.roll(cur, step, 1), cur)
    for q in range(BLOCK // 16):
        if q:
            cur = pltpu.roll(cur, 16, 1)
        out_ref[0, 16 * q : 16 * (q + 1), :] = cur.astype(jnp.bfloat16)
    out_ref[0, :, :BLOCK] = jnp.zeros((BLOCK, BLOCK), jnp.bfloat16)


def strips(taps):
    groups, length = taps.shape
    width = length + BLOCK
    return pl.pallas_call(
        strip_kernel,
        grid=(groups,),
        in_specs=[pl.BlockSpec((groups, length), lambda g: (0, 0))],
        out_specs=pl.BlockSpec((1, BLOCK, width), lambda g: (g, 0, 0)),
        out_shape=jax.ShapeDtypeStruct((groups, BLOCK, width), jnp.bfloat16),
        compiler_params=params(),
        cost_estimate=LONG,
    )(taps)


def in_order(order_ref, source, target, sems):
    return [
        pltpu.make_async_copy(source.at[d], target.at[order_ref[d]], sems.at[d])
        for d in range(source.shape[0])
    ]


def start(made):
    for copy in made:
        copy.start()


def wait(made):
    for copy in made:
        copy.wait()


def rows_of(group):
    first = GROUP * group
    return pl.ds(first if isinstance(first, int) else pl.multiple_of(first, GROUP), GROUP)


def filters_kernel(order_ref, x_hbm, strip_hbm, out_hbm, x, strip, out, acc, x_sem, s_sem, out_sem):
    groups = strip.shape[0]
    arrive = in_order(order_ref, x_hbm, x, x_sem)
    start(arrive)
    for g in range(groups):
        pltpu.make_async_copy(strip_hbm.at[g], strip.at[g], s_sem.at[g]).start()
    wait(arrive)

    @pl.loop(0, groups)
    def _(g):
        pltpu.make_async_copy(strip_hbm.at[g], strip.at[g], s_sem.at[g]).wait()
        filter_group(False, g, 0, x, strip, out, acc.at[0])
        filter_group(True, g, groups, x, strip, out, acc.at[1])

    leave = [
        pltpu.make_async_copy(out.at[order_ref[d]], out_hbm.at[d], out_sem.at[d])
        for d in range(out.shape[0])
    ]
    start(leave)
    wait(leave)


def filter_group(backward, g, shift, x, strip, out, acc):
    pieces = x.shape[0]
    pairs = pieces // 2
    wide = 2 * BLOCK
    nothing = jnp.zeros((GROUP, wide), jnp.bfloat16)
    rows = rows_of(g + shift)
    blocks = [
        jnp.concatenate([x[2 * i, rows, :], x[2 * i + 1, rows, :]], axis=1)
        for i in range(pairs)
    ]
    for lag in range(0, pairs, SPAN):
        at = BLOCK + wide * lag
        lefts, weights = [], []
        for k in range(min(SPAN, pairs - lag)):
            if backward:
                froms = range(lag + k, pairs + k)
            else:
                froms = range(-k, pairs - lag - k)
            lefts.append(
                jnp.concatenate(
                    [blocks[i] if 0 <= i < pairs else nothing for i in froms], axis=0
                )
            )
            weights += [
                strip[g, :, at + wide * k : at + wide * (k + 1)],
                strip[g, :, at + wide * k - BLOCK : at + wide * k + BLOCK],
            ]
        if backward:
            ends = at + wide * min(SPAN, pairs - lag)
            weights = [strip[g, :, at:ends], strip[g, :, at - BLOCK : ends - BLOCK]]
        part = dot(
            jnp.concatenate(lefts, axis=1),
            jnp.concatenate(weights, axis=0),
            NT if backward else NN,
        )
        depth = GROUP * (pairs - lag)
        if lag == 0:
            acc[...] = part
        elif backward:
            acc[:depth, :] += part
        else:
            acc[GROUP * lag :, :] += part
    for i in range(pairs):
        both = acc[rows_of(i), :].astype(jnp.bfloat16)
        out[2 * i, rows, :] = both[:, :BLOCK]
        out[2 * i + 1, rows, :] = both[:, BLOCK:]


def filters(order, x, strip):
    pieces = x.shape[0]
    groups = strip.shape[0]
    rows = GROUP * pieces // 2
    anywhere = pl.BlockSpec(memory_space=pl.ANY)
    return pl.pallas_call(
        filters_kernel,
        in_specs=[pl.BlockSpec(memory_space=pltpu.SMEM), anywhere, anywhere],
        out_specs=anywhere,
        scratch_shapes=[
            pltpu.VMEM(x.shape, x.dtype),
            pltpu.VMEM(strip.shape, strip.dtype),
            pltpu.VMEM(x.shape, x.dtype),
            pltpu.VMEM((2, rows, 2 * BLOCK), jnp.float32),
            pltpu.SemaphoreType.DMA((pieces,)),
            pltpu.SemaphoreType.DMA((groups,)),
            pltpu.SemaphoreType.DMA((pieces,)),
        ],
        out_shape=pltpu.HBM(x.shape, x.dtype),
        compiler_params=params(40),
        cost_estimate=LONG,
    )(order, x, pltpu.with_memory_space_constraint(strip, pltpu.HBM))


def lag_kernel(order_ref, x_hbm, out_ref, x, squares, sums, x_sem):
    pieces = x.shape[0]
    groups = out_ref.shape[0]
    total = GROUP * pieces
    last = BLOCK - 1
    arrive = in_order(order_ref, x_hbm, x, x_sem)
    start(arrive)
    row = lax.broadcasted_iota(jnp.int32, (BLOCK, BLOCK), 0)
    col = lax.broadcasted_iota(jnp.int32, (BLOCK, BLOCK), 1)
    mirror = jnp.where(row + col == last, 1.0, 0.0).astype(jnp.bfloat16)
    nothing = jnp.zeros((GROUP, BLOCK), jnp.bfloat16)
    for i in range(2):
        squares[i, :, pieces * BLOCK :] = jnp.zeros((BLOCK, BLOCK), jnp.float32)
    wait(arrive)
    def one(g, here):
        xs = jnp.concatenate([x[j, rows_of(g), :] for j in range(pieces)], axis=0)
        x_turned = dot(mirror, xs, NT).astype(jnp.bfloat16)
        blocks = [x[j, rows_of(g + groups), :] for j in range(pieces)]
        for lag in range(0, pieces, 2):
            depth = total - GROUP * lag // BLOCK * BLOCK
            right = jnp.concatenate(
                [
                    jnp.concatenate(
                        [
                            blocks[j] if j < pieces else nothing
                            for j in range(first, first + depth // GROUP)
                        ],
                        axis=0,
                    )
                    for first in (lag, lag + 1)
                ],
                axis=1,
            )
            squares[here, :, lag * BLOCK : (lag + 2) * BLOCK] = dot(
                x_turned[:, :depth], right, NN
            )
        step = 8
        for t in range(0, pieces, step):
            cols = slice(t * BLOCK, (t + step + 1) * BLOCK)
            added = None
            for q in range(BLOCK // 8):
                moved = pltpu.roll(
                    squares[here, 8 * q : 8 * q + 8, cols], 8 * q, 1, stride=1, stride_axis=0
                )
                added = moved if added is None else added + moved
            added = jnp.sum(added, axis=0, keepdims=True)
            skip = BLOCK if t else 0
            sums[pl.ds(g, 1), t * BLOCK + skip : (t + step + 1) * BLOCK] = added[:, skip:]

    @pl.loop(0, groups // AT_ONCE)
    def _(i):
        for k in range(AT_ONCE):
            one(i * AT_ONCE + k, k % 2)

    width = sums.shape[1]
    out_ref[...] = pltpu.roll(sums[...], width - last, 1)[:, : pieces * BLOCK].astype(jnp.bfloat16)


def lag_sums_of(order, x, groups):
    pieces = x.shape[0]
    length = pieces * BLOCK
    return pl.pallas_call(
        lag_kernel,
        in_specs=[
            pl.BlockSpec(memory_space=pltpu.SMEM),
            pl.BlockSpec(memory_space=pl.ANY),
        ],
        out_specs=pl.BlockSpec(memory_space=pltpu.VMEM),
        scratch_shapes=[
            pltpu.VMEM(x.shape, x.dtype),
            pltpu.VMEM((2, BLOCK, length + BLOCK), jnp.float32),
            pltpu.VMEM((groups, length + BLOCK), jnp.float32),
            pltpu.SemaphoreType.DMA((pieces,)),
        ],
        out_shape=jax.ShapeDtypeStruct((groups, length), jnp.bfloat16),
        compiler_params=params(),
        cost_estimate=SHORT,
    )(order, pltpu.with_memory_space_constraint(x, pltpu.HBM))


def post_kernel(r_hbm, *refs):
    ins, outs = refs[:4], refs[4:8]
    r, here, made, r_sem, in_sem, out_sem = refs[8], refs[9:13], refs[13:17], *refs[17:]
    into = list(
        zip(
            tile_copies(r_hbm, r, r_sem, CHUNKS),
            *[copies(ins[k], here[k], in_sem.at[k], CHUNKS) for k in range(4)],
            strict=True,
        )
    )
    leave = list(
        zip(*[copies(made[k], outs[k], out_sem.at[k], CHUNKS) for k in range(4)], strict=True)
    )
    for group in into:
        start(group)
    tiles = r.shape[0] // CHUNKS
    for i in range(CHUNKS):
        wait(into[i])
        for t in range(i * tiles, (i + 1) * tiles):
            cols = slice(t * BLOCK, (t + 1) * BLOCK)
            for half in range(2):
                turned = r[t, half * BLOCK : (half + 1) * BLOCK, :].T
                for k in (2 * half, 2 * half + 1):
                    made[k][0, :, cols] = product_of(here[k][0, :, cols], turned)
        start(leave[i])
    for group in leave:
        wait(group)


def post(r, *factors):
    anywhere = pl.BlockSpec(memory_space=pl.ANY)
    a = factors[0]
    return pl.pallas_call(
        post_kernel,
        in_specs=[anywhere] * 5,
        out_specs=[anywhere] * 4,
        out_shape=[jax.ShapeDtypeStruct(a.shape, a.dtype)] * 4,
        scratch_shapes=[pltpu.VMEM(r.shape, r.dtype)]
        + [pltpu.VMEM(a.shape, a.dtype)] * 8
        + [
            pltpu.SemaphoreType.DMA((CHUNKS,)),
            pltpu.SemaphoreType.DMA((4, CHUNKS)),
            pltpu.SemaphoreType.DMA((4, CHUNKS)),
        ],
        compiler_params=params(40),
        cost_estimate=pl.CostEstimate(
            flops=4 * a.size, bytes_accessed=20 * a.size, transcendentals=0
        ),
    )(r, *[pltpu.with_memory_space_constraint(a, pltpu.HBM) for a in factors])


def taps_kernel(sequences, taps_ref, mine_ref, others_ref, out_ref):
    taps = taps_ref[...]
    length = taps.shape[1]
    root = jnp.sqrt(jnp.mean(taps * taps, axis=1, keepdims=True) + EPSILON)
    scale = 1.0 / (math.sqrt(length) * root)
    mean = (mine_ref[...] + others_ref[...]) / sequences
    projection = jnp.sum(mean * taps, axis=1, keepdims=True)
    out_ref[...] = scale * mean - taps * (scale * scale * scale) * projection


def taps_grad_of(taps, mine, others, sequences):
    return pl.pallas_call(
        functools.partial(taps_kernel, sequences),
        out_shape=jax.ShapeDtypeStruct(taps.shape, jnp.float32),
        compiler_params=params(16),
    )(taps, mine, others)


def exchange(tiles):
    return lax.all_to_all(tiles, "ctx", split_axis=0, concat_axis=0, tiled=True)


def from_partner(x, step):
    return lax.ppermute(x, "dp", [(i, i ^ step) for i in range(lax.axis_size("dp"))])


def shards(output_gate_input, key_input, value_input, upstream, filter_taps, order):
    sequences = lax.axis_size("dp")
    arrived = exchange(pre(key_input, value_input, upstream, output_gate_input))
    strip = strips(filter_taps)
    filtered = filters(order, arrived, strip)
    returned = exchange(filtered)
    arrived, _ = lax.optimization_barrier((arrived, filtered))
    lag_sums = lag_sums_of(order, arrived, filter_taps.shape[0])
    near = [from_partner(lag_sums, step) for step in range(1, sequences // 2)]
    half = sum((part.astype(jnp.float32) for part in near), lag_sums.astype(jnp.float32))
    far = from_partner(half, sequences // 2)
    mixed_out, gate_grad, key_grad, value_grad = post(
        returned, output_gate_input, upstream, value_input, key_input
    )
    taps_grad = taps_grad_of(filter_taps, half, far, sequences)
    return mixed_out, gate_grad, key_grad, value_grad, taps_grad


def solution(mesh):
    rows = P("dp", "ctx", None)
    return jax.shard_map(
        shards,
        mesh=mesh,
        in_specs=(rows, rows, rows, rows, P("ctx", None), P()),
        out_specs=(rows, rows, rows, rows, P("ctx", None)),
        check_vma=False,
    )
```
